512 devices in a mesh: batch: 16 (over y, core), proto: 32 (over x, z).
Axes of the slice: x: 4, y: 8, z: 8, core: 2. Of those that a mesh axis runs over, the one named last changes fastest.
Arguments:
- embeddings: bfloat16 [4096, 2, 768], P('batch'), may hold values from -6 to 6
- prototypes: bfloat16 [65536, 768], P(('batch', 'proto')), may hold values from -6 to 6
Outputs:
- grad_embed: bfloat16 [4096, 2, 768], P(('batch', 'proto'))
- grad_proto: bfloat16 [65536, 768], P(('batch', 'proto'))
The draws below stay inside these ranges and needn't reach their ends.
All inputs are finite; a program needn't handle non-finite values.
Results may differ from the reference program's by a relative error of at most 0.019.
Values may be sent and summed in bfloat16 or wider, within the bound.
No kernel may reach another device: no remote copies, remote signals or barrier semaphores. Data moves between devices by JAX's collectives and lax.ppermute only.
A program may use at most 64 MiB of HBM per device.

```python
import jax
import jax.numpy as jnp
from jax import lax

D = 768
PROTOS = 65536
ITERS = 3
BATCH = 4096
N_BATCH = 16
N_PROTO = 32


cluster_count = 64


def shared_parts(key):
    directions = jax.random.normal(jax.random.fold_in(key, 101), (cluster_count, D), jnp.float32)
    return directions


def draw_embeddings(key, part):
    directions = shared_parts(key)
    key = jax.random.fold_in(key, 1)
    pick_keys = jax.random.split(key, 5)
    wide_pick = jax.random.randint(pick_keys[0], (BATCH,), 0, cluster_count)
    narrow_pick = jax.random.randint(pick_keys[1], (BATCH,), cluster_count // 2, 3 * cluster_count // 4)
    chooser = jax.random.randint(pick_keys[2], (BATCH,), 0, 2)
    cluster = jnp.where(chooser == 0, wide_pick, narrow_pick)
    strength = jnp.exp(jax.random.uniform(pick_keys[3], (BATCH, 1, 1), jnp.float32, jnp.log(0.3), jnp.log(2.0)))
    centre = directions[cluster][:, None, :]
    jitter = jax.random.normal(pick_keys[4], (BATCH, 2, D), jnp.float32)
    values = (strength * centre + jitter) / jnp.sqrt(1.0 + strength * strength)
    return jnp.clip(values, -6.0, 6.0).astype(jnp.bfloat16)


def draw_prototypes(key, part):
    directions = shared_parts(key)
    key = jax.random.fold_in(key, 2)
    pick_keys = jax.random.split(key, 5)
    wide_pick = jax.random.randint(pick_keys[0], (PROTOS,), 0, cluster_count)
    narrow_pick = jax.random.randint(pick_keys[1], (PROTOS,), 0, cluster_count // 4)
    chooser = jax.random.randint(pick_keys[2], (PROTOS,), 0, 2)
    cluster = jnp.where(chooser == 0, wide_pick, narrow_pick)
    strength = jnp.exp(jax.random.uniform(pick_keys[3], (PROTOS, 1), jnp.float32, jnp.log(0.3), jnp.log(2.0)))
    centre = directions[cluster]
    jitter = jax.random.normal(pick_keys[4], (PROTOS, D), jnp.float32)
    values = (strength * centre + jitter) / jnp.sqrt(1.0 + strength * strength)
    return jnp.clip(values, -6.0, 6.0).astype(jnp.bfloat16)


def setup_inputs(seed: int = 0) -> dict:
    splits = jax.random.split(jax.random.key(seed), 3)
    embeddings = draw_embeddings(jax.random.fold_in(splits[2], 71), 0)
    prototypes = draw_prototypes(jax.random.fold_in(splits[2], 71), 0)
    return {"embeddings": embeddings, "prototypes": prototypes}


sharpness_divisor = 0.1
entropy = 0.05
loss_factor = 16.0

def unit_rows(values):
    widened = values.astype(jnp.float32)
    return (widened * lax.rsqrt(lax.optimization_barrier(jnp.sum(widened * widened, axis=-1, keepdims=True)) + 1e-06)).astype(jnp.bfloat16)

def reference(embeddings, prototypes):
    batch_rows = embeddings.shape[0]
    block_size = PROTOS // N_PROTO
    normed = unit_rows(embeddings)
    flat_rows = normed.reshape(batch_rows * 2, D)
    centers = unit_rows(prototypes)
    blocks = centers.reshape(N_BATCH, N_PROTO, block_size // N_BATCH, D).transpose(1, 0, 2, 3).reshape(N_PROTO, block_size, D)

    def scores_of(shard_piece):
        return jnp.dot(flat_rows, shard_piece.T, preferred_element_type=jnp.float32).reshape(batch_rows, 2, block_size)
    scale_rows = jnp.ones((batch_rows, 2), jnp.float32)
    exponent_sum = jnp.zeros((batch_rows, 2), jnp.float32)
    weights_all = jnp.zeros((N_PROTO, 2, block_size), jnp.float32)
    for sweep_index in range(ITERS):

        def visit_block(state_pair, shard_piece):
            rowsum, weighted_likelihood_sum = state_pair
            prototype_logits = scores_of(shard_piece)
            plan_exp = jnp.exp(prototype_logits / entropy)
            colsum = lax.optimization_barrier(jnp.sum(scale_rows[:, :, None] * plan_exp, axis=0))
            weights = 1.0 / (PROTOS * colsum)
            rowsum = rowsum + lax.optimization_barrier(jnp.sum(plan_exp * weights[None], axis=2))
            if sweep_index == 0:
                weighted_likelihood_sum = weighted_likelihood_sum + lax.optimization_barrier(jnp.sum(jnp.exp(prototype_logits / sharpness_divisor), axis=2))
            return ((rowsum, weighted_likelihood_sum), weights)
        zeros_pair = jnp.zeros((batch_rows, 2), jnp.float32)
        (rowsum, exponent_sum), weights_all = lax.scan(visit_block, (zeros_pair, exponent_sum), blocks)
        scale_rows = 1.0 / (batch_rows * rowsum)

    def finish_block(grad_rows, block_pair):
        shard_piece, weights = block_pair
        prototype_logits = scores_of(shard_piece)
        code_targets = batch_rows * scale_rows[:, :, None] * jnp.exp(prototype_logits / entropy) * weights[None]
        predicted_likelihoods = jnp.exp(prototype_logits / sharpness_divisor) / exponent_sum[:, :, None]
        score_gradient = (loss_factor / sharpness_divisor * (predicted_likelihoods - code_targets[:, ::-1, :])).astype(jnp.bfloat16)
        flat_grad = score_gradient.reshape(batch_rows * 2, block_size)
        partial_value = jnp.dot(flat_grad, shard_piece, preferred_element_type=jnp.float32).astype(jnp.bfloat16)
        grad_rows = grad_rows + partial_value.astype(jnp.float32)
        shard_grad = flat_grad.reshape(N_BATCH, batch_rows * 2 // N_BATCH, block_size).astype(jnp.float32)
        shard_rows = flat_rows.reshape(N_BATCH, batch_rows * 2 // N_BATCH, D).astype(jnp.float32)
        proto_terms = jnp.einsum('nrk,nrd->nkd', shard_grad, shard_rows).astype(jnp.bfloat16)
        return (grad_rows, lax.optimization_barrier(jnp.sum(proto_terms.astype(jnp.float32), axis=0)).astype(jnp.bfloat16))
    grad_rows, proto_blocks = lax.scan(finish_block, jnp.zeros((batch_rows * 2, D), jnp.float32), (blocks, weights_all))
    grad_embed = grad_rows.astype(jnp.bfloat16).reshape(batch_rows, 2, D)
    grad_proto = proto_blocks.reshape(N_PROTO, N_BATCH, block_size // N_BATCH, D).transpose(1, 0, 2, 3).reshape(PROTOS, D)
    return (grad_embed, grad_proto)
```

```python
import jax
import jax.numpy as jnp
from jax import lax
from jax.sharding import Mesh, PartitionSpec as P

PROTOS = 65536
CLIPS = 4096
CORES, XS, ZS = 2, 4, 8
SCALE = 16.0 / 0.1


def unit_rows(values):
    widened = values.astype(jnp.float32)
    norm = lax.rsqrt(jnp.sum(widened * widened, axis=-1, keepdims=True) + 1e-06)
    return (widened * norm).astype(jnp.bfloat16)


def sum_over(part, axes, count):
    everyone = jnp.broadcast_to(part[None], (count,) + part.shape)
    return jnp.sum(lax.all_to_all(everyone, axes, 0, 0), axis=0)


def swap_cores(part):
    return lax.ppermute(part, "core", [(0, 1), (1, 0)])


def on_device(embeddings, prototypes):
    clips = embeddings.shape[0]
    width = embeddings.shape[2]
    ys = lax.axis_size("y")
    first = lax.axis_index("core") == 0

    centers = lax.all_gather(unit_rows(prototypes), "y", axis=0, tiled=True)
    mine = unit_rows(embeddings).transpose(1, 0, 2)
    rows = jnp.concatenate([mine, swap_cores(mine)], axis=1)
    protos = centers.shape[0]

    scores = lax.dot_general(
        rows, centers, (((2,), (1,)), ((), ())), preferred_element_type=jnp.float32
    )
    likely = jnp.exp(scores * 10.0)

    def col_scale(weighted):
        part = jnp.sum(weighted, axis=1)
        return 1.0 / (PROTOS * sum_over(part, "y", ys))

    def row_sums(parts):
        parts = parts.reshape(-1, 2, 2, clips)
        parts = jnp.where(first, parts, parts[:, :, ::-1])
        total = sum_over(parts, ("x", "z", "core"), XS * ZS * CORES)
        return jnp.where(first, total, total[:, :, ::-1]).reshape(-1, 2, 2 * clips)

    col = col_scale(likely * likely)
    both = row_sums(
        jnp.stack([jnp.sum(likely * likely * col[:, None, :], axis=2), jnp.sum(likely, axis=2)])
    )
    row, soft = 1.0 / (CLIPS * both[0]), both[1]
    for _ in range(2):
        col = col_scale(likely * likely * row[:, :, None])
        row = 1.0 / (CLIPS * row_sums(jnp.sum(likely * likely * col[:, None, :], axis=2)[None])[0])

    probs = likely * (SCALE / soft)[:, :, None]
    codes = likely * likely * (SCALE * CLIPS * row)[:, :, None] * col[:, None, :]
    grad = (probs - codes[::-1]).astype(jnp.bfloat16)

    grad_proto = lax.psum_scatter(
        lax.dot_general(
            grad, rows, (((0, 1), (0, 1)), ((), ())), preferred_element_type=jnp.float32
        ).astype(jnp.bfloat16),
        "y",
        scatter_dimension=0,
        tiled=True,
    )
    part = lax.dot_general(
        grad, centers, (((2,), (0,)), ((), ())), preferred_element_type=jnp.float32
    ).astype(jnp.bfloat16)
    part = part[:, :clips].astype(jnp.float32) + swap_cores(part[:, clips:]).astype(jnp.float32)
    part = part.astype(jnp.bfloat16).reshape(2, XS, clips // XS, width).transpose(1, 0, 2, 3)
    part = jnp.sum(lax.all_to_all(part, "x", 0, 0).astype(jnp.float32), axis=0)
    part = part.astype(jnp.bfloat16).reshape(2, ZS, clips // XS // ZS, width).transpose(1, 0, 2, 3)
    part = jnp.sum(lax.all_to_all(part, "z", 0, 0).astype(jnp.float32), axis=0)
    grad_embed = part.astype(jnp.bfloat16).transpose(1, 0, 2)
    return grad_embed, grad_proto


def solution(mesh):
    split = Mesh(mesh.devices.reshape(-1, CORES, XS, ZS), ("y", "core", "x", "z"))
    batch, every = ("y", "core"), ("y", "core", "x", "z")
    return jax.shard_map(
        on_device,
        mesh=split,
        in_specs=(P(batch, None, None), P(every, None)),
        out_specs=(P(every, None, None), P(every, None)),
        check_vma=False,
    )
```

```python
import functools

import jax
import jax.numpy as jnp
from jax import lax
from jax.experimental import pallas as pl
from jax.experimental.pallas import tpu as pltpu
from jax.sharding import Mesh, PartitionSpec as P

PROTOS = 65536
CLIPS = 4096
YS, CORES, XS, ZS = 8, 2, 4, 8
SCALE = 16.0 / 0.1
F32, BF16 = jnp.float32, jnp.bfloat16
LANES = 128
WIDTH = 768
RING = (0, 2, -2, 1, 3, -1, -3, 4)
MINE = 256
ROWS = CORES * MINE
COLS = len(RING) * LANES
GROUP = XS * ZS * CORES


def params():
    return pltpu.CompilerParams(
        dimension_semantics=("arbitrary",), vmem_limit_bytes=28 * 1024 * 1024
    )


def call(kernel, places, ins, in_blocks, outs, out_blocks, grid, scratch, flops):
    return pl.pallas_call(
        kernel,
        out_shape=outs,
        grid_spec=pltpu.PrefetchScalarGridSpec(
            num_scalar_prefetch=1,
            grid=(grid,),
            in_specs=in_blocks,
            out_specs=out_blocks,
            scratch_shapes=scratch,
        ),
        compiler_params=params(),
        cost_estimate=pl.CostEstimate(flops=flops, bytes_accessed=4 << 20, transcendentals=0),
    )(places, *ins)


def whole(shape):
    return pl.BlockSpec(shape, lambda g, s: (0,) * len(shape))


def turned(block):
    return jnp.sum(block.T, axis=0, keepdims=True)


def down(row):
    return jnp.broadcast_to(row, (LANES, LANES)).T


def clip_row(s, view, half, part):
    return view * 4 + jnp.bitwise_xor(s[0], half) * 2 + part


def unit_kernel(x_ref, o_ref):
    wide = x_ref[...].astype(F32)
    norm = lax.rsqrt(jnp.sum(wide * wide, axis=-1, keepdims=True) + 1e-06)
    o_ref[...] = (wide * norm).astype(BF16)


def put_clips(s, step, acc, out):
    view, half = step // 2, step % 2
    for part in range(2):
        block = acc[part * LANES : (part + 1) * LANES]
        out[pl.ds(clip_row(s, view, half, part), 1), :] = turned(block)


def put_cols(s, cols, out):
    for view in range(2):
        for slot in range(len(RING)):
            out[pl.ds(view * YS + s[1 + slot], 1), :] = cols[
                view : view + 1, slot * LANES : (slot + 1) * LANES
            ]


def col_scales(s, recv_ref, total, cols):
    total[...] = jnp.sum(recv_ref[...], axis=0)
    for view in range(2):
        for slot in range(len(RING)):
            value = total[pl.ds(view * YS + s[1 + slot], 1), :]
            cols[view : view + 1, slot * LANES : (slot + 1) * LANES] = 1.0 / (PROTOS * value)


def score_kernel(s, rows, c0, c1, c2, up, dn, ft, fe, e_ref, cols_ref, soft_ref, centers, cols, soft):
    step = pl.program_id(0)

    @pl.when(step == 0)
    def _():
        place = 0
        for piece in (c0, c1, c2, up, dn, ft, fe):
            count = piece.shape[0]
            centers[place : place + count] = piece[...]
            place += count
        cols[...] = jnp.zeros_like(cols)

    scores = lax.dot_general(
        rows[0], centers[...], (((1,), (1,)), ((), ())), preferred_element_type=F32
    )
    likely = jnp.exp(scores * 10.0)
    e_ref[0] = likely
    acc = likely[:, :LANES]
    for slot in range(1, len(RING)):
        acc = acc + likely[:, slot * LANES : (slot + 1) * LANES]
    put_clips(s, step, acc, soft)
    view = step // 2
    cols[pl.ds(view, 1), :] += jnp.sum(likely * likely, axis=0, keepdims=True)

    @pl.when(step == 3)
    def _():
        soft_ref[...] = soft[...]
        put_cols(s, cols[...], soft)
        cols_ref[...] = jnp.broadcast_to(soft[...][None], cols_ref.shape)


def row_kernel(first, s, e_ref, recv_ref, *refs):
    if first:
        soft_ref, out_ref, total, cols, sums = refs
    else:
        out_ref, total, cols, sums = refs
    step = pl.program_id(0)

    @pl.when(step == 0)
    def _():
        col_scales(s, recv_ref, total, cols)

    view = step // 2
    scale = cols[pl.ds(view, 1), :]
    acc = None
    for slot in range(len(RING)):
        lanes = slice(slot * LANES, (slot + 1) * LANES)
        likely = e_ref[0, :, lanes]
        term = likely * likely * scale[:, lanes]
        acc = term if acc is None else acc + term
    put_clips(s, step, acc, sums)

    @pl.when(step == 3)
    def _():
        if first:
            both = jnp.concatenate([sums[...], soft_ref[...][:8]]).astype(BF16)
        else:
            both = sums[...]
        out_ref[...] = jnp.broadcast_to(both[None], out_ref.shape)


def col_kernel(first, s, e_ref, recv_ref, *refs):
    if first:
        out_ref, soft_ref, total, cols, sums = refs
    else:
        out_ref, total, cols, sums = refs
    step = pl.program_id(0)

    @pl.when(step == 0)
    def _():
        total[...] = jnp.sum(recv_ref[...].astype(F32), axis=0)
        cols[...] = jnp.zeros_like(cols)
        if first:
            soft_ref[...] = total[8:]

    view, half = step // 2, step % 2
    part_sums = []
    scale = [
        down(1.0 / (CLIPS * total[pl.ds(clip_row(s, view, half, part), 1), :])) for part in range(2)
    ]
    scale = jnp.concatenate(scale)
    for slot in range(len(RING)):
        likely = e_ref[0, :, slot * LANES : (slot + 1) * LANES]
        part_sums.append(jnp.sum(likely * likely * scale, axis=0, keepdims=True))
    cols[pl.ds(view, 1), :] += jnp.concatenate(part_sums, axis=1)

    @pl.when(step == 3)
    def _():
        put_cols(s, cols[...], sums)
        out_ref[...] = jnp.broadcast_to(sums[...][None], out_ref.shape)


def grad_kernel(
    s, e_ref, row_ref, col_ref, soft_ref, c0, c1, c2, up, dn, ft, fe,
    g_ref, mine_ref, other_ref, total, clips, cols, centers,
):
    step = pl.program_id(0)

    @pl.when(step == 0)
    def _():
        col_scales(s, col_ref, total, cols)
        clips[...] = jnp.sum(row_ref[...], axis=0)
        place = 0
        for piece in (c0, c1, c2, up, dn, ft, fe):
            count = piece.shape[0]
            centers[place : place + count] = piece[...]
            place += count

    block = (step + 2) % 4
    half, part = block // 2, block % 2
    for view in range(2):
        soft = down(SCALE / soft_ref[pl.ds(clip_row(s, view, half, part), 1), :])
        code = clips[pl.ds(clip_row(s, 1 - view, half, part), 1), :]
        code = down(SCALE * CLIPS / (CLIPS * code))
        for slot in range(len(RING)):
            lanes = slice(slot * LANES, (slot + 1) * LANES)
            mine, swapped = e_ref[view, :, lanes], e_ref[1 - view, :, lanes]
            codes = swapped * swapped * code * cols[1 - view : 2 - view, lanes]
            g_ref[view, :, lanes] = (mine * soft - codes).astype(BF16)
    for view in range(2):
        out = jnp.dot(g_ref[view], centers[...], preferred_element_type=F32).astype(BF16)

        @pl.when(step < 2)
        def _(out=out, view=view):
            other_ref[view] = out

        @pl.when(step >= 2)
        def _(out=out, view=view):
            mine_ref[view] = out


def proto_kernel(s, rows_ref, g_ref, rest_ref, up_ref, dn_ref, far_ref):
    step = pl.program_id(0)
    out = jnp.dot(rows_ref[:, :ROWS], g_ref[0], preferred_element_type=F32)
    out = out + jnp.dot(rows_ref[:, ROWS:], g_ref[1], preferred_element_type=F32)
    out = out.astype(BF16)
    one, two = out[:, :LANES], out[:, LANES:]

    @pl.when(step == 0)
    def _():
        rest_ref[0] = one
        rest_ref[1] = two

    @pl.when(step == 1)
    def _():
        rest_ref[2] = one
        up_ref[0] = two

    @pl.when(step == 2)
    def _():
        up_ref[1] = one
        dn_ref[0] = two

    @pl.when(step == 3)
    def _():
        dn_ref[1] = one
        far_ref[0] = two[: WIDTH // 2]
        far_ref[1] = two[WIDTH // 2 :]


def shift(part, axis, size, by):
    return lax.ppermute(part, axis, [(i, (i + by) % size) for i in range(size)])


def add(*parts):
    total = parts[0].astype(F32)
    for part in parts[1:]:
        total = total + part.astype(F32)
    return total.astype(BF16)


def gather_y(shard):
    below = shift(shard, "y", YS, 2)
    above = shift(shard, "y", YS, -2)
    up = shift(jnp.concatenate([shard, above]), "y", YS, -1)
    dn = shift(jnp.concatenate([shard, below]), "y", YS, 1)
    half = shard.shape[0] // 2
    far_top = shift(above[:half], "y", YS, -2)
    far_end = shift(below[half:], "y", YS, 2)
    return shard, above, below, up, dn, far_top, far_end


def scatter_y(rest, up, dn, far):
    below = shift(up, "y", YS, 1)
    above = shift(dn, "y", YS, -1)
    far_below = shift(far[0], "y", YS, 2)
    far_above = shift(far[1], "y", YS, -2)
    half = WIDTH // 2
    plus = add(rest[1], below[1], jnp.pad(far_below, ((0, half), (0, 0))))
    minus = add(rest[2], above[1], jnp.pad(far_above, ((half, 0), (0, 0))))
    return add(rest[0], below[0], above[0], shift(plus, "y", YS, 2), shift(minus, "y", YS, -2))


def unit_rows(values):
    wide = values.astype(F32)
    norm = lax.rsqrt(jnp.sum(wide * wide, axis=-1, keepdims=True) + 1e-06)
    return (wide * norm).astype(BF16)


def on_device(embeddings, prototypes):
    y, core = lax.axis_index("y"), lax.axis_index("core")
    places = jnp.stack([core] + [lax.rem(y + d + YS, YS) for d in RING]).astype(jnp.int32)

    theirs = shift(embeddings, "core", CORES, 1)
    shard = pl.pallas_call(
        unit_kernel,
        out_shape=jax.ShapeDtypeStruct(prototypes.shape, BF16),
        compiler_params=pltpu.CompilerParams(vmem_limit_bytes=28 * 1024 * 1024),
    )(prototypes)
    pieces = gather_y(shard)
    piece_blocks = [whole(p.shape) for p in pieces]
    rows = jnp.concatenate(
        [unit_rows(embeddings).transpose(1, 0, 2), unit_rows(theirs).transpose(1, 0, 2)], axis=1
    )
    flat = rows.reshape(2 * ROWS, WIDTH).T

    e_shape = jax.ShapeDtypeStruct((2, ROWS, COLS), F32)
    e_block = pl.BlockSpec((1, MINE, COLS), lambda g, s: (g // 2, g % 2, 0))
    col_shape = jax.ShapeDtypeStruct((YS, 2 * YS, LANES), F32)
    row_shape = jax.ShapeDtypeStruct((GROUP, 8, LANES), F32)
    both_shape = jax.ShapeDtypeStruct((GROUP, 16, LANES), BF16)
    col_scratch = pltpu.VMEM((2 * YS, LANES), F32)
    row_scratch = pltpu.VMEM((8, LANES), F32)
    cols = pltpu.VMEM((2, COLS), F32)
    vpu = 4 * ROWS * COLS

    likely, col_part, soft = call(
        score_kernel, places, (rows, *pieces),
        [pl.BlockSpec((1, MINE, WIDTH), lambda g, s: (g // 2, g % 2, 0)), *piece_blocks],
        (e_shape, col_shape, jax.ShapeDtypeStruct((2 * YS, LANES), F32)),
        (e_block, whole(col_shape.shape), whole((2 * YS, LANES))),
        4, [pltpu.VMEM((COLS, WIDTH), BF16), cols, col_scratch], 4 * ROWS * COLS * WIDTH,
    )

    def y_sum(part):
        return lax.all_to_all(part, "y", 0, 0)

    def xzc_sum(part):
        return lax.all_to_all(part, ("x", "z", "core"), 0, 0)

    col_part = y_sum(col_part)
    row_part = call(
        functools.partial(row_kernel, True), places, (likely, col_part, soft),
        [e_block, whole(col_shape.shape), whole((2 * YS, LANES))],
        both_shape, whole(both_shape.shape), 4, [col_scratch, cols, row_scratch], vpu,
    )
    row_part = xzc_sum(row_part)
    col_part, soft = call(
        functools.partial(col_kernel, True), places, (likely, row_part),
        [e_block, whole(both_shape.shape)],
        (col_shape, jax.ShapeDtypeStruct((8, LANES), F32)),
        (whole(col_shape.shape), whole((8, LANES))),
        4, [col_scratch, cols, col_scratch], vpu,
    )
    for sweep in range(2):
        col_part = y_sum(col_part)
        row_part = call(
            functools.partial(row_kernel, False), places, (likely, col_part),
            [e_block, whole(col_shape.shape)],
            row_shape, whole(row_shape.shape), 4, [col_scratch, cols, row_scratch], vpu,
        )
        row_part = xzc_sum(row_part)
        if sweep == 0:
            col_part = call(
                functools.partial(col_kernel, False), places, (likely, row_part),
                [e_block, whole(row_shape.shape)],
                col_shape, whole(col_shape.shape), 4, [row_scratch, cols, col_scratch], vpu,
            )

    block = (2, LANES, WIDTH)
    half_shape = jax.ShapeDtypeStruct((2, MINE, WIDTH), BF16)
    grad, mine, other = call(
        grad_kernel, places, (likely, row_part, col_part, soft, *pieces),
        [
            pl.BlockSpec((2, LANES, COLS), lambda g, s: (0, (g + 2) % 4, 0)),
            whole(row_shape.shape), whole(col_shape.shape), whole((8, LANES)), *piece_blocks,
        ],
        (jax.ShapeDtypeStruct((2, ROWS, COLS), BF16), half_shape, half_shape),
        (
            pl.BlockSpec((2, LANES, COLS), lambda g, s: (0, (g + 2) % 4, 0)),
            pl.BlockSpec(block, lambda g, s: (0, jnp.maximum(g - 2, 0), 0)),
            pl.BlockSpec(block, lambda g, s: (0, jnp.minimum(g, 1), 0)),
        ),
        4, [col_scratch, row_scratch, cols, pltpu.VMEM((COLS, WIDTH), BF16)],
        4 * ROWS * COLS * WIDTH,
    )
    theirs = shift(other, "core", CORES, 1)
    out_shapes = [(3, WIDTH, LANES), (2, WIDTH, LANES), (2, WIDTH, LANES), (2, WIDTH // 2, LANES)]
    sums = call(
        proto_kernel, places, (flat, grad),
        [whole(flat.shape), pl.BlockSpec((2, ROWS, 2 * LANES), lambda g, s: (0, 0, g))],
        tuple(jax.ShapeDtypeStruct(shape, BF16) for shape in out_shapes),
        tuple(whole(shape) for shape in out_shapes),
        4, [], 4 * ROWS * COLS * WIDTH,
    )
    grad_proto = scatter_y(*sums).T

    part = add(mine, theirs).reshape(2, XS, MINE // XS, WIDTH).transpose(1, 0, 2, 3)
    part = jnp.sum(lax.all_to_all(part, "x", 0, 0).astype(F32), axis=0).astype(BF16)
    part = part.reshape(2, ZS, MINE // XS // ZS, WIDTH).transpose(1, 0, 2, 3)
    part = jnp.sum(lax.all_to_all(part, "z", 0, 0).astype(F32), axis=0).astype(BF16)
    return part.transpose(1, 0, 2), grad_proto


def solution(mesh):
    split = Mesh(mesh.devices.reshape(YS, CORES, XS, ZS), ("y", "core", "x", "z"))
    batch, every = ("y", "core"), ("y", "core", "x", "z")
    return jax.shard_map(
        on_device,
        mesh=split,
        in_specs=(P(batch, None, None), P(every, None)),
        out_specs=(P(every, None, None), P(every, None)),
        check_vma=False,
    )
```

```python
import functools

import jax
import jax.numpy as jnp
from jax import lax
from jax.experimental import pallas as pl
from jax.experimental.pallas import tpu as pltpu
from jax.sharding import Mesh, PartitionSpec as P

PROTOS = 65536
CLIPS = 4096
YS, CORES, XS, ZS = 8, 2, 4, 8
SCALE = 16.0 / 0.1
F32, BF16 = jnp.float32, jnp.bfloat16
LANES = 128
WIDTH = 768
RING = (0, 1, -1, 2, -2, -3, 3, 4)
EARLY = 6
MINE = 256
ROWS = CORES * MINE
SPLIT = EARLY * LANES
COLS = len(RING) * LANES
GROUP = XS * ZS * CORES
VIEWS = 2
BLOCKS = [(view, half) for view in range(VIEWS) for half in range(CORES)]


def call(kernel, ins, outs, scratch=(), flops=4 * ROWS * COLS):
    scalars = 1 if ins[0].dtype == jnp.int32 else 0
    blocks = [pl.BlockSpec(memory_space=pltpu.SMEM)] * scalars
    blocks += [pl.BlockSpec(memory_space=pltpu.VMEM)] * (len(ins) - scalars)
    out_blocks = [pl.BlockSpec(memory_space=pltpu.VMEM)] * len(outs)
    return pl.pallas_call(
        kernel,
        out_shape=[jax.ShapeDtypeStruct(shape, dtype) for shape, dtype in outs],
        in_specs=blocks,
        out_specs=out_blocks,
        scratch_shapes=[pltpu.VMEM(shape, dtype) for shape, dtype in scratch],
        compiler_params=pltpu.CompilerParams(vmem_limit_bytes=16 * 1024 * 1024),
        cost_estimate=pl.CostEstimate(flops=flops, bytes_accessed=2 << 20, transcendentals=0),
    )(*ins)


def turned(block):
    return jnp.sum(block.T, axis=0, keepdims=True)


def down(row):
    return jnp.broadcast_to(row, (LANES, LANES)).T


def lanes_of(slot):
    return slice(slot * LANES, (slot + 1) * LANES)


def clips_of(half):
    return slice(half * MINE, (half + 1) * MINE)


def clip_row(s, view, half, part):
    return view * 4 + jnp.bitwise_xor(s[0], half) * 2 + part


def put_clips(s, view, half, acc, out):
    for part in range(2):
        block = acc[part * LANES : (part + 1) * LANES]
        out[pl.ds(clip_row(s, view, half, part), 1), :] = turned(block)


def clip_scale(s, view, half, ref, scale):
    rows = [ref[pl.ds(clip_row(s, view, half, part), 1), :] for part in range(2)]
    return jnp.concatenate([down(scale / row) for row in rows])


def put_cols(s, view, slot, value, out):
    out[pl.ds(view * YS + s[1 + slot], 1), :] = value


def col_scale(s, view, slot, ref):
    return 1.0 / (PROTOS * ref[pl.ds(view * YS + s[1 + slot], 1), :])


def copies(ref, value):
    ref[...] = jnp.broadcast_to(value[None], ref.shape)


def units(values):
    wide = values.astype(F32)
    norm = lax.rsqrt(jnp.sum(wide * wide, axis=-1, keepdims=True) + 1e-06)
    return (wide * norm).astype(BF16)


def unit_kernel(x_ref, o_ref):
    o_ref[...] = units(x_ref[...])


def rows_kernel(mine_ref, theirs_ref, rows_ref, flat_ref):
    for half, ref in enumerate((mine_ref, theirs_ref)):
        for view in range(VIEWS):
            unit = units(ref[view])
            rows_ref[view, clips_of(half)] = unit
            start = (half * VIEWS + view) * MINE
            flat_ref[:, start : start + MINE] = unit.T


def score(s, slots, rows, pieces, e_ref, centers, part, soft):
    for place, piece in enumerate(pieces):
        centers[lanes_of(place)] = piece[...]
    for view in range(VIEWS):
        acc = None
        for chunk in range(0, len(slots), 2):
            lanes = slice(chunk * LANES, (chunk + 2) * LANES)
            scores = lax.dot_general(
                rows[view], centers[lanes], (((1,), (1,)), ((), ())), preferred_element_type=F32
            )
            likely = jnp.exp(scores * 10.0)
            e_ref[view, :, lanes] = likely
            sums = jnp.sum(likely * likely, axis=0, keepdims=True)
            put_cols(s, view, slots[chunk], sums[:, :LANES], part)
            put_cols(s, view, slots[chunk + 1], sums[:, LANES:], part)
            both = likely[:, :LANES] + likely[:, LANES:]
            acc = both if acc is None else acc + both
        for half in range(CORES):
            put_clips(s, view, half, acc[clips_of(half)], soft)


def early_kernel(s, rows, *refs):
    pieces, (e_ref, part, soft, centers) = refs[:EARLY], refs[EARLY:]
    part[...] = jnp.zeros_like(part)
    score(s, range(EARLY), rows, pieces, e_ref, centers, part, soft)


def late_kernel(s, rows, *refs):
    late = len(RING) - EARLY
    pieces, (early_part, early_soft, e_ref, cols_ref, soft_ref, centers, part, soft) = (
        refs[:late],
        refs[late:],
    )
    part[...] = jnp.zeros_like(part)
    score(s, range(EARLY, len(RING)), rows, pieces, e_ref, centers, part, soft)
    soft_ref[...] = early_soft[...] + soft[...]
    copies(cols_ref, early_part[...] + part[...])


def likely_of(e_refs, view, rows, slot):
    early, late = e_refs
    return early[view, rows, lanes_of(slot)] if slot < EARLY else late[view, rows, lanes_of(slot - EARLY)]


def row_kernel(first, s, early, late, recv_ref, *refs):
    if first:
        soft_ref, out_ref, total, sums = refs
    else:
        out_ref, total, sums = refs
    total[...] = jnp.sum(recv_ref[...], axis=0)
    for view, half in BLOCKS:
        acc = None
        for slot in range(len(RING)):
            likely = likely_of((early, late), view, clips_of(half), slot)
            term = likely * likely * col_scale(s, view, slot, total)
            acc = term if acc is None else acc + term
        put_clips(s, view, half, acc, sums)
    both = sums[...]
    if first:
        both = jnp.concatenate([both, soft_ref[...]]).astype(BF16)
    copies(out_ref, both)


def col_kernel(first, s, early, late, recv_ref, *refs):
    if first:
        out_ref, soft_ref, total, sums = refs
    else:
        out_ref, total, sums = refs
    total[...] = jnp.sum(recv_ref[...].astype(F32), axis=0)
    if first:
        soft_ref[...] = total[8:]
    for view in range(VIEWS):
        scale = [clip_scale(s, view, half, total, 1.0 / CLIPS) for half in range(CORES)]
        scale = jnp.concatenate(scale)
        for slot in range(len(RING)):
            likely = likely_of((early, late), view, slice(None), slot)
            value = jnp.sum(likely * likely * scale, axis=0, keepdims=True)
            put_cols(s, view, slot, value, sums)
    copies(out_ref, sums[...])


def grad_kernel(
    s, early, late, row_ref, col_ref, soft_ref, near_centers, far_centers,
    mine_ref, other_ref, grads, total, clips,
):
    total[...] = jnp.sum(col_ref[...], axis=0)
    clips[...] = jnp.sum(row_ref[...], axis=0)
    for half, ref in ((1, other_ref), (0, mine_ref)):
        rows = clips_of(half)
        code = [clip_scale(s, view, half, clips, SCALE) for view in range(VIEWS)]
        start = half * VIEWS * MINE
        for view in range(VIEWS):
            soft = clip_scale(s, view, half, soft_ref, SCALE)
            for slot in range(len(RING)):
                likely = likely_of((early, late), view, rows, slot)
                swapped = likely_of((early, late), 1 - view, rows, slot)
                scale = col_scale(s, 1 - view, slot, total)
                value = likely * soft - swapped * swapped * code[1 - view] * scale
                place = start + view * MINE
                grads[place : place + MINE, lanes_of(slot)] = value.astype(BF16)
        part = slice(start, start + VIEWS * MINE)
        out = jnp.dot(grads[part, :SPLIT], near_centers[...], preferred_element_type=F32)
        out = out + jnp.dot(grads[part, SPLIT:], far_centers[...], preferred_element_type=F32)
        for place in range(XS * ZS):
            eight = [out[view * MINE + place * 8 : view * MINE + place * 8 + 8] for view in range(2)]
            ref[place] = jnp.concatenate(eight).astype(BF16)


def proto_kernel(flat_ref, grads, *outs):
    for chunk in range(0, len(RING), 2):
        lanes = slice(chunk * LANES, (chunk + 2) * LANES)
        out = jnp.dot(flat_ref[...], grads[:, lanes], preferred_element_type=F32).astype(BF16)
        outs[chunk][...] = out[:, :LANES]
        outs[chunk + 1][...] = out[:, LANES:]


def last_kernel(own, one, two, out_ref):
    total = own[...].astype(F32) + one[...].astype(F32) + two[...].astype(F32)
    out_ref[...] = total.T.astype(BF16)


def shift(part, axis, size, by):
    return lax.ppermute(part, axis, [(i, (i + by) % size) for i in range(size)])


def add(*parts):
    total = parts[0].astype(F32)
    for part in parts[1:]:
        total = total + part.astype(F32)
    return total.astype(BF16)


def swap(part, side):
    low = [(y + side) % YS for y in range(0, YS, 2)]
    pairs = [(y, (y + 1) % YS) for y in low]
    return lax.ppermute(part, "y", pairs + [(b, a) for a, b in pairs])


def gather_y(shard):
    pieces, one, two = [shard], shard, shard
    for _ in range(3):
        one, two = swap(two, 0), swap(one, 1)
        pieces += [one, two]
    return *pieces[:5], two, one, swap(two, 0)


def scatter_y(own, *sums):
    one, two = sums[5], add(sums[4], swap(sums[6], 0))
    for at in (2, 0):
        one, two = add(sums[at], swap(two, 1)), add(sums[at + 1], swap(one, 0))
    (out,) = call(last_kernel, (own, swap(one, 0), swap(two, 1)), [((LANES, WIDTH), BF16)])
    return out


def y_sums(part):
    return lax.all_to_all(part, "y", 0, 0)


def group_sums(part):
    return lax.all_to_all(part, ("x", "z", "core"), 0, 0)


def on_device(embeddings, prototypes):
    y, core = lax.axis_index("y"), lax.axis_index("core")
    sign = 1 - 2 * lax.rem(y, 2)
    places = jnp.stack([core] + [lax.rem(y + sign * d + YS, YS) for d in RING]).astype(jnp.int32)

    (shard,) = call(unit_kernel, (prototypes,), [(prototypes.shape, BF16)])
    mine, shard = lax.optimization_barrier((embeddings.transpose(1, 0, 2), shard))
    theirs = shift(mine, "core", CORES, 1)
    pieces = gather_y(shard)
    rows, flat = call(
        rows_kernel,
        (mine, theirs),
        [((VIEWS, ROWS, WIDTH), BF16), ((WIDTH, VIEWS * ROWS), BF16)],
    )

    cols, rows8, rows16 = ((16, LANES), F32), ((8, LANES), F32), ((16, LANES), F32)
    col_out = ((YS, 16, LANES), F32)
    row_out = ((GROUP, 8, LANES), F32)
    both_out = ((GROUP, 16, LANES), BF16)
    work = 4 * ROWS * WIDTH
    early, col_part, soft, near_centers = call(
        early_kernel, (places, rows, *pieces[:EARLY]),
        [((VIEWS, ROWS, SPLIT), F32), cols, rows8, ((SPLIT, WIDTH), BF16)], (), work * SPLIT,
    )
    late, col_part, soft, far_centers = call(
        late_kernel, (places, rows, *pieces[EARLY:], col_part, soft),
        [((VIEWS, ROWS, COLS - SPLIT), F32), col_out, rows8, ((COLS - SPLIT, WIDTH), BF16)],
        [cols, rows8], work * (COLS - SPLIT),
    )
    col_part = y_sums(col_part)
    (row_part,) = call(
        functools.partial(row_kernel, True), (places, early, late, col_part, soft), [both_out],
        [cols, rows8],
    )
    row_part = group_sums(row_part)
    col_part, soft = call(
        functools.partial(col_kernel, True), (places, early, late, row_part), [col_out, rows8],
        [rows16, cols],
    )
    col_part = y_sums(col_part)
    (row_part,) = call(
        functools.partial(row_kernel, False), (places, early, late, col_part), [row_out], [cols, rows8]
    )
    row_part = group_sums(row_part)
    (col_part,) = call(
        functools.partial(col_kernel, False), (places, early, late, row_part), [col_out], [rows8, cols]
    )
    col_part = y_sums(col_part)
    (row_part,) = call(
        functools.partial(row_kernel, False), (places, early, late, col_part), [row_out], [cols, rows8]
    )
    row_part = group_sums(row_part)

    ge_out = ((XS * ZS, 16, WIDTH), BF16)
    mine, other, grads = call(
        grad_kernel,
        (places, early, late, row_part, col_part, soft, near_centers, far_centers),
        [ge_out, ge_out, ((VIEWS * ROWS, COLS), BF16)], [cols, rows8], work * COLS,
    )
    sums = call(
        proto_kernel, (flat, grads), [((WIDTH, LANES), BF16)] * len(RING), (), work * COLS
    )
    part = add(mine, shift(other, "core", CORES, 1))
    grad_proto = scatter_y(*sums)
    part = lax.all_to_all(part, ("x", "z"), 0, 0)
    part = jnp.sum(part.astype(F32), axis=0).astype(BF16)
    return part.reshape(2, 8, WIDTH).transpose(1, 0, 2), grad_proto


def solution(mesh):
    split = Mesh(mesh.devices.reshape(YS, CORES, XS, ZS), ("y", "core", "x", "z"))
    batch, every = ("y", "core"), ("y", "core", "x", "z")
    return jax.shard_map(
        on_device,
        mesh=split,
        in_specs=(P(batch, None, None), P(every, None)),
        out_specs=(P(every, None, None), P(every, None)),
        check_vma=False,
    )
```

```python
import functools

import jax
import jax.numpy as jnp
from jax import lax
from jax.experimental import pallas as pl
from jax.experimental.layout import Layout, with_layout_constraint
from jax.experimental.pallas import tpu as pltpu
from jax.sharding import Mesh, PartitionSpec as P

PROTOS = 65536
CLIPS = 4096
YS, CORES, XS, ZS = 8, 2, 4, 8
SCALE = 16.0 / 0.1
F32, BF16 = jnp.float32, jnp.bfloat16
LANES = 128
WIDTH = 768
RING = (0, 1, -1, 2, -2, -3, 3, 4)
EARLY = 6
MINE = 256
ROWS = CORES * MINE
SPLIT = EARLY * LANES
COLS = len(RING) * LANES
GROUP = XS * ZS * CORES
VIEWS = 2
BLOCKS = [(view, half) for view in range(VIEWS) for half in range(CORES)]


def call(kernel, ins, outs, scratch=(), flops=4 * ROWS * COLS):
    return pl.pallas_call(
        kernel,
        out_shape=[jax.ShapeDtypeStruct(shape, dtype) for shape, dtype in outs],
        in_specs=[pl.BlockSpec(memory_space=pltpu.VMEM)] * len(ins),
        out_specs=[pl.BlockSpec(memory_space=pltpu.VMEM)] * len(outs),
        scratch_shapes=[pltpu.VMEM(shape, dtype) for shape, dtype in scratch],
        compiler_params=pltpu.CompilerParams(vmem_limit_bytes=16 * 1024 * 1024),
        cost_estimate=pl.CostEstimate(flops=flops, bytes_accessed=2 << 20, transcendentals=0),
    )(*ins)


def places():
    y, core = lax.axis_index("y"), lax.axis_index("core")
    sign = 1 - 2 * lax.rem(y, 2)
    return [core] + [lax.rem(y + sign * d + YS, YS) for d in RING]


def turned(block):
    return jnp.sum(block.T, axis=0, keepdims=True)


def down(row):
    return jnp.broadcast_to(row, (LANES, LANES)).T


def lanes_of(slot):
    return slice(slot * LANES, (slot + 1) * LANES)


def clips_of(half):
    return slice(half * MINE, (half + 1) * MINE)


def clip_row(s, view, half, part):
    return view * 4 + jnp.bitwise_xor(s[0], half) * 2 + part


def put_clips(s, view, half, acc, out):
    for part in range(2):
        block = acc[part * LANES : (part + 1) * LANES]
        out[pl.ds(clip_row(s, view, half, part), 1), :] = turned(block)


def clip_scale(s, view, half, ref, scale):
    rows = [ref[pl.ds(clip_row(s, view, half, part), 1), :] for part in range(2)]
    return jnp.concatenate([down(scale / row) for row in rows])


def put_cols(s, view, slot, value, out):
    out[pl.ds(view * YS + s[1 + slot], 1), :] = value


def col_scale(s, view, slot, ref):
    return 1.0 / (PROTOS * ref[pl.ds(view * YS + s[1 + slot], 1), :])


def copies(ref, value):
    ref[...] = jnp.broadcast_to(value[None], ref.shape)


def units(values):
    wide = values.astype(F32)
    norm = lax.rsqrt(jnp.sum(wide * wide, axis=-1, keepdims=True) + 1e-06)
    return (wide * norm).astype(BF16)


def unit_kernel(x_ref, o_ref):
    o_ref[...] = units(x_ref[...])


def rows_kernel(mine_ref, theirs_ref, rows_ref, flat_ref):
    for half, ref in enumerate((mine_ref, theirs_ref)):
        for view in range(VIEWS):
            unit = units(ref[view])
            rows_ref[view, clips_of(half)] = unit
            start = (half * VIEWS + view) * MINE
            flat_ref[:, start : start + MINE] = unit.T


def score(s, slots, rows, pieces, e_ref, centers, part, soft):
    for place, piece in enumerate(pieces):
        centers[lanes_of(place)] = piece[...]
    for view in range(VIEWS):
        acc = None
        for chunk in range(0, len(slots), 2):
            lanes = slice(chunk * LANES, (chunk + 2) * LANES)
            scores = lax.dot_general(
                rows[view], centers[lanes], (((1,), (1,)), ((), ())), preferred_element_type=F32
            )
            likely = jnp.exp(scores * 10.0)
            e_ref[view, :, lanes] = likely
            sums = jnp.sum(likely * likely, axis=0, keepdims=True)
            put_cols(s, view, slots[chunk], sums[:, :LANES], part)
            put_cols(s, view, slots[chunk + 1], sums[:, LANES:], part)
            both = likely[:, :LANES] + likely[:, LANES:]
            acc = both if acc is None else acc + both
        for half in range(CORES):
            put_clips(s, view, half, acc[clips_of(half)], soft)


def early_kernel(rows, *refs):
    s = places()
    pieces, (e_ref, part, soft, centers) = refs[:EARLY], refs[EARLY:]
    part[...] = jnp.zeros_like(part)
    score(s, range(EARLY), rows, pieces, e_ref, centers, part, soft)


def late_kernel(rows, *refs):
    s = places()
    late = len(RING) - EARLY
    pieces, (early_part, early_soft, e_ref, cols_ref, soft_ref, centers, part, soft) = (
        refs[:late],
        refs[late:],
    )
    part[...] = jnp.zeros_like(part)
    score(s, range(EARLY, len(RING)), rows, pieces, e_ref, centers, part, soft)
    soft_ref[...] = early_soft[...] + soft[...]
    copies(cols_ref, early_part[...] + part[...])


def likely_of(e_refs, view, rows, slot):
    early, late = e_refs
    return early[view, rows, lanes_of(slot)] if slot < EARLY else late[view, rows, lanes_of(slot - EARLY)]


def row_kernel(first, early, late, recv_ref, *refs):
    s = places()
    if first:
        soft_ref, out_ref, total, sums = refs
    else:
        out_ref, total, sums = refs
    total[...] = jnp.sum(recv_ref[...], axis=0)
    for view, half in BLOCKS:
        acc = None
        for slot in range(len(RING)):
            likely = likely_of((early, late), view, clips_of(half), slot)
            term = likely * likely * col_scale(s, view, slot, total)
            acc = term if acc is None else acc + term
        put_clips(s, view, half, acc, sums)
    both = sums[...]
    if first:
        both = jnp.concatenate([both, soft_ref[...]]).astype(BF16)
    copies(out_ref, both)


def col_kernel(first, early, late, recv_ref, *refs):
    s = places()
    if first:
        out_ref, soft_ref, total, sums = refs
    else:
        out_ref, total, sums = refs
    total[...] = jnp.sum(recv_ref[...].astype(F32), axis=0)
    if first:
        soft_ref[...] = total[8:]
    for view in range(VIEWS):
        scale = [clip_scale(s, view, half, total, 1.0 / CLIPS) for half in range(CORES)]
        scale = jnp.concatenate(scale)
        for slot in range(len(RING)):
            likely = likely_of((early, late), view, slice(None), slot)
            value = jnp.sum(likely * likely * scale, axis=0, keepdims=True)
            put_cols(s, view, slot, value, sums)
    copies(out_ref, sums[...])


def grad_kernel(
    early, late, row_ref, col_ref, soft_ref, near_centers, far_centers,
    mine_ref, other_ref, grads, total, clips,
):
    s = places()
    total[...] = jnp.sum(col_ref[...], axis=0)
    clips[...] = jnp.sum(row_ref[...], axis=0)
    for half, ref in ((1, other_ref), (0, mine_ref)):
        rows = clips_of(half)
        code = [clip_scale(s, view, half, clips, SCALE) for view in range(VIEWS)]
        start = half * VIEWS * MINE
        for view in range(VIEWS):
            soft = clip_scale(s, view, half, soft_ref, SCALE)
            for slot in range(len(RING)):
                likely = likely_of((early, late), view, rows, slot)
                swapped = likely_of((early, late), 1 - view, rows, slot)
                scale = col_scale(s, 1 - view, slot, total)
                value = likely * soft - swapped * swapped * code[1 - view] * scale
                place = start + view * MINE
                grads[place : place + MINE, lanes_of(slot)] = value.astype(BF16)
        part = slice(start, start + VIEWS * MINE)
        out = jnp.dot(grads[part, :SPLIT], near_centers[...], preferred_element_type=F32)
        out = out + jnp.dot(grads[part, SPLIT:], far_centers[...], preferred_element_type=F32)
        for place in range(XS * ZS):
            eight = [out[view * MINE + place * 8 : view * MINE + place * 8 + 8] for view in range(2)]
            ref[place] = jnp.concatenate(eight).astype(BF16)


def proto_kernel(flat_ref, grads, *outs):
    for chunk in range(0, len(RING), 2):
        lanes = slice(chunk * LANES, (chunk + 2) * LANES)
        out = jnp.dot(flat_ref[...], grads[:, lanes], preferred_element_type=F32).astype(BF16)
        outs[chunk][...] = out[:, :LANES]
        outs[chunk + 1][...] = out[:, LANES:]


def last_kernel(own, one, two, out_ref):
    total = own[...].astype(F32) + one[...].astype(F32) + two[...].astype(F32)
    out_ref[...] = total.T.astype(BF16)


def shift(part, axis, size, by):
    return lax.ppermute(part, axis, [(i, (i + by) % size) for i in range(size)])


def add(*parts):
    total = parts[0].astype(F32)
    for part in parts[1:]:
        total = total + part.astype(F32)
    return total.astype(BF16)


def swap(part, side):
    low = [(y + side) % YS for y in range(0, YS, 2)]
    pairs = [(y, (y + 1) % YS) for y in low]
    return lax.ppermute(part, "y", pairs + [(b, a) for a, b in pairs])


def gather_y(shard):
    pieces, one, two = [shard], shard, shard
    for _ in range(3):
        one, two = swap(two, 0), swap(one, 1)
        pieces += [one, two]
    return *pieces[:5], two, one, swap(two, 0)


def scatter_y(own, *sums):
    one, two = sums[5], add(sums[4], swap(sums[6], 0))
    for at in (2, 0):
        one, two = add(sums[at], swap(two, 1)), add(sums[at + 1], swap(one, 0))
    (out,) = call(last_kernel, (own, swap(one, 0), swap(two, 1)), [((LANES, WIDTH), BF16)])
    return out


def y_sums(part):
    return lax.all_to_all(part, "y", 0, 0)


def group_sums(part):
    return lax.all_to_all(part, ("x", "z", "core"), 0, 0)


def on_device(embeddings, prototypes):
    (shard,) = call(unit_kernel, (prototypes,), [(prototypes.shape, BF16)])
    mine = embeddings.transpose(1, 0, 2)
    as_given = Layout(major_to_minor=(0, 1, 2))
    theirs = shift(with_layout_constraint(embeddings, as_given), "core", CORES, 1)
    theirs = with_layout_constraint(theirs, as_given).transpose(1, 0, 2)
    pieces = gather_y(shard)
    rows, flat = call(
        rows_kernel,
        (mine, theirs),
        [((VIEWS, ROWS, WIDTH), BF16), ((WIDTH, VIEWS * ROWS), BF16)],
    )
    cols, rows8, rows16 = ((16, LANES), F32), ((8, LANES), F32), ((16, LANES), F32)
    col_out = ((YS, 16, LANES), F32)
    row_out = ((GROUP, 8, LANES), F32)
    both_out = ((GROUP, 16, LANES), BF16)
    work = 4 * ROWS * WIDTH
    early, col_part, soft, near_centers = call(
        early_kernel, (rows, *pieces[:EARLY]),
        [((VIEWS, ROWS, SPLIT), F32), cols, rows8, ((SPLIT, WIDTH), BF16)], (), work * SPLIT,
    )
    late, col_part, soft, far_centers = call(
        late_kernel, (rows, *pieces[EARLY:], col_part, soft),
        [((VIEWS, ROWS, COLS - SPLIT), F32), col_out, rows8, ((COLS - SPLIT, WIDTH), BF16)],
        [cols, rows8], work * (COLS - SPLIT),
    )
    col_part = y_sums(col_part)
    (row_part,) = call(
        functools.partial(row_kernel, True), (early, late, col_part, soft), [both_out],
        [cols, rows8],
    )
    row_part = group_sums(row_part)
    col_part, soft = call(
        functools.partial(col_kernel, True), (early, late, row_part), [col_out, rows8],
        [rows16, cols],
    )
    col_part = y_sums(col_part)
    (row_part,) = call(
        functools.partial(row_kernel, False), (early, late, col_part), [row_out], [cols, rows8]
    )
    row_part = group_sums(row_part)
    (col_part,) = call(
        functools.partial(col_kernel, False), (early, late, row_part), [col_out], [rows8, cols]
    )
    col_part = y_sums(col_part)
    (row_part,) = call(
        functools.partial(row_kernel, False), (early, late, col_part), [row_out], [cols, rows8]
    )
    row_part = group_sums(row_part)

    ge_out = ((XS * ZS, 16, WIDTH), BF16)
    mine, other, grads = call(
        grad_kernel,
        (early, late, row_part, col_part, soft, near_centers, far_centers),
        [ge_out, ge_out, ((VIEWS * ROWS, COLS), BF16)], [cols, rows8], work * COLS,
    )
    sums = call(
        proto_kernel, (flat, grads), [((WIDTH, LANES), BF16)] * len(RING), (), work * COLS
    )
    part = add(mine, shift(other, "core", CORES, 1))
    part = lax.all_to_all(part, ("x", "z"), 0, 0)
    part = jnp.sum(part.astype(F32), axis=0).astype(BF16)
    grad_embed = part.reshape(2, 8, WIDTH).transpose(1, 0, 2)
    own, grad_embed = lax.optimization_barrier((sums[0], grad_embed))
    return grad_embed, scatter_y(own, *sums[1:])


def solution(mesh):
    split = Mesh(mesh.devices.reshape(YS, CORES, XS, ZS), ("y", "core", "x", "z"))
    batch, every = ("y", "core"), ("y", "core", "x", "z")
    return jax.shard_map(
        on_device,
        mesh=split,
        in_specs=(P(batch, None, None), P(every, None)),
        out_specs=(P(every, None, None), P(every, None)),
        check_vma=False,
    )
```

```python
import functools

import jax
import jax.numpy as jnp
from jax import lax
from jax.experimental import pallas as pl
from jax.experimental.layout import Layout, with_layout_constraint
from jax.experimental.pallas import tpu as pltpu
from jax.sharding import Mesh, PartitionSpec as P

PROTOS = 65536
CLIPS = 4096
YS, CORES, XS, ZS = 8, 2, 4, 8
SCALE = 16.0 / 0.1
F32, BF16 = jnp.float32, jnp.bfloat16
LANES = 128
WIDTH = 768
SLOTS = 8
EARLY = 6
MINE = 256
ROWS = CORES * MINE
SPLIT = EARLY * LANES
COLS = SLOTS * LANES
GROUP = XS * ZS * CORES
VIEWS = 2
BLOCKS = [(view, half) for view in range(VIEWS) for half in range(CORES)]


def call(kernel, ins, outs, scratch=(), flops=4 * ROWS * COLS):
    return pl.pallas_call(
        kernel,
        out_shape=[jax.ShapeDtypeStruct(shape, dtype) for shape, dtype in outs],
        in_specs=[pl.BlockSpec(memory_space=pltpu.VMEM)] * len(ins),
        out_specs=[pl.BlockSpec(memory_space=pltpu.VMEM)] * len(outs),
        scratch_shapes=[pltpu.VMEM(shape, dtype) for shape, dtype in scratch],
        compiler_params=pltpu.CompilerParams(vmem_limit_bytes=16 * 1024 * 1024),
        cost_estimate=pl.CostEstimate(flops=flops, bytes_accessed=2 << 20, transcendentals=0),
    )(*ins)


def sides():
    y, core = lax.axis_index("y"), lax.axis_index("core")
    return 1 - 2 * lax.rem(y + core, 2), 1 - 2 * lax.rem(y // 2 + core, 2)


def places():
    y, (one, two) = lax.axis_index("y"), sides()
    steps = (0, one, -one, 2 * two, -2 * two, -3 * one, 3 * one, 4)
    return [lax.axis_index("core")] + [lax.rem(y + step + YS, YS) for step in steps]


def turned(block):
    return jnp.sum(block.T, axis=0, keepdims=True)


def down(row):
    return jnp.broadcast_to(row, (LANES, LANES)).T


def lanes_of(slot):
    return slice(slot * LANES, (slot + 1) * LANES)


def clips_of(half):
    return slice(half * MINE, (half + 1) * MINE)


def clip_row(s, view, half, part):
    return view * 4 + jnp.bitwise_xor(s[0], half) * 2 + part


def put_clips(s, view, half, acc, out):
    for part in range(2):
        block = acc[part * LANES : (part + 1) * LANES]
        out[pl.ds(clip_row(s, view, half, part), 1), :] = turned(block)


def clip_scale(s, view, half, ref, scale):
    rows = [ref[pl.ds(clip_row(s, view, half, part), 1), :] for part in range(2)]
    return jnp.concatenate([down(scale / row) for row in rows])


def put_cols(s, view, slot, value, out):
    out[pl.ds(view * YS + s[1 + slot], 1), :] = value


def col_scale(s, view, slot, ref):
    return 1.0 / (PROTOS * ref[pl.ds(view * YS + s[1 + slot], 1), :])


def copies(ref, value):
    ref[...] = jnp.broadcast_to(value[None], ref.shape)


def units(values):
    wide = values.astype(F32)
    norm = lax.rsqrt(jnp.sum(wide * wide, axis=-1, keepdims=True) + 1e-06)
    return (wide * norm).astype(BF16)


def rows_kernel(mine_ref, theirs_ref, rows_ref, flat_ref):
    for half, ref in enumerate((mine_ref, theirs_ref)):
        for view in range(VIEWS):
            unit = units(ref[view])
            rows_ref[view, clips_of(half)] = unit
            start = (half * VIEWS + view) * MINE
            flat_ref[:, start : start + MINE] = unit.T


def score(s, slots, rows, pieces, e_ref, centers, part, soft):
    for place, piece in enumerate(pieces):
        centers[lanes_of(place)] = units(piece[...])
    for view in range(VIEWS):
        acc = None
        for chunk in range(0, len(slots), 2):
            lanes = slice(chunk * LANES, (chunk + 2) * LANES)
            scores = lax.dot_general(
                rows[view], centers[lanes], (((1,), (1,)), ((), ())), preferred_element_type=F32
            )
            likely = jnp.exp(scores * 10.0)
            e_ref[view, :, lanes] = likely
            sums = jnp.sum(likely * likely, axis=0, keepdims=True)
            put_cols(s, view, slots[chunk], sums[:, :LANES], part)
            put_cols(s, view, slots[chunk + 1], sums[:, LANES:], part)
            both = likely[:, :LANES] + likely[:, LANES:]
            acc = both if acc is None else acc + both
        for half in range(CORES):
            put_clips(s, view, half, acc[clips_of(half)], soft)


def early_kernel(rows, *refs):
    s = places()
    pieces, (e_ref, part, soft, centers) = refs[:EARLY], refs[EARLY:]
    part[...] = jnp.zeros_like(part)
    score(s, range(EARLY), rows, pieces, e_ref, centers, part, soft)


def late_kernel(rows, *refs):
    s = places()
    late = SLOTS - EARLY
    pieces, (early_part, early_soft, e_ref, cols_ref, soft_ref, centers, part, soft) = (
        refs[:late],
        refs[late:],
    )
    part[...] = jnp.zeros_like(part)
    score(s, range(EARLY, SLOTS), rows, pieces, e_ref, centers, part, soft)
    soft_ref[...] = early_soft[...] + soft[...]
    copies(cols_ref, early_part[...] + part[...])


def likely_of(e_refs, view, rows, slot):
    early, late = e_refs
    return early[view, rows, lanes_of(slot)] if slot < EARLY else late[view, rows, lanes_of(slot - EARLY)]


def row_kernel(first, early, late, recv_ref, *refs):
    s = places()
    if first:
        soft_ref, out_ref, total, sums = refs
    else:
        out_ref, total, sums = refs
    total[...] = jnp.sum(recv_ref[...], axis=0)
    for view, half in BLOCKS:
        acc = None
        for slot in range(SLOTS):
            likely = likely_of((early, late), view, clips_of(half), slot)
            term = likely * likely * col_scale(s, view, slot, total)
            acc = term if acc is None else acc + term
        put_clips(s, view, half, acc, sums)
    both = sums[...]
    if first:
        both = jnp.concatenate([both, soft_ref[...]]).astype(BF16)
    copies(out_ref, both)


def col_kernel(first, early, late, recv_ref, *refs):
    s = places()
    if first:
        out_ref, soft_ref, total, sums = refs
    else:
        out_ref, total, sums = refs
    total[...] = jnp.sum(recv_ref[...].astype(F32), axis=0)
    if first:
        soft_ref[...] = total[8:]
    for view in range(VIEWS):
        scale = [clip_scale(s, view, half, total, 1.0 / CLIPS) for half in range(CORES)]
        scale = jnp.concatenate(scale)
        for slot in range(SLOTS):
            likely = likely_of((early, late), view, slice(None), slot)
            value = jnp.sum(likely * likely * scale, axis=0, keepdims=True)
            put_cols(s, view, slot, value, sums)
    copies(out_ref, sums[...])


def grad_kernel(
    early, late, row_ref, col_ref, soft_ref, near_centers, far_centers,
    mine_ref, other_ref, grads, total, clips,
):
    s = places()
    total[...] = jnp.sum(col_ref[...], axis=0)
    clips[...] = jnp.sum(row_ref[...], axis=0)
    for half, ref in ((1, other_ref), (0, mine_ref)):
        rows = clips_of(half)
        code = [clip_scale(s, view, half, clips, SCALE) for view in range(VIEWS)]
        start = half * VIEWS * MINE
        for view in range(VIEWS):
            soft = clip_scale(s, view, half, soft_ref, SCALE)
            for slot in range(SLOTS):
                likely = likely_of((early, late), view, rows, slot)
                swapped = likely_of((early, late), 1 - view, rows, slot)
                scale = col_scale(s, 1 - view, slot, total)
                value = likely * soft - swapped * swapped * code[1 - view] * scale
                place = start + view * MINE
                grads[place : place + MINE, lanes_of(slot)] = value.astype(BF16)
        part = slice(start, start + VIEWS * MINE)
        out = jnp.dot(grads[part, :SPLIT], near_centers[...], preferred_element_type=F32)
        out = out + jnp.dot(grads[part, SPLIT:], far_centers[...], preferred_element_type=F32)
        for place in range(XS * ZS):
            eight = [out[view * MINE + place * 8 : view * MINE + place * 8 + 8] for view in range(2)]
            ref[place] = jnp.concatenate(eight).astype(BF16)


def proto_kernel(flat_ref, grads, *outs):
    for chunk in range(0, SLOTS, 2):
        lanes = slice(chunk * LANES, (chunk + 2) * LANES)
        out = jnp.dot(flat_ref[...], grads[:, lanes], preferred_element_type=F32).astype(BF16)
        outs[chunk][...] = out[:, :LANES]
        outs[chunk + 1][...] = out[:, LANES:]


def last_kernel(own, *refs):
    *parts, out_ref = refs
    total = own[...].astype(F32)
    for part in parts:
        total = total + part[...].astype(F32)
    out_ref[...] = total.T.astype(BF16)


def shift(part, axis, size, by):
    return lax.ppermute(part, axis, [(i, (i + by) % size) for i in range(size)])


def add(*parts):
    total = parts[0].astype(F32)
    for part in parts[1:]:
        total = total + part.astype(F32)
    return total.astype(BF16)


def swap(part, side, by):
    pairs = []
    for core in range(CORES):
        for y in range(YS):
            if (y // by) % 2 == (side + core) % 2:
                one, two = y * CORES + core, (y + by) % YS * CORES + core
                pairs += [(one, two), (two, one)]
    return lax.ppermute(part, ("y", "core"), pairs)


def gather_y(shard):
    one, two = sides()
    up1, dn1 = swap(shard, 0, 1), swap(shard, 1, 1)
    up2, dn2 = swap(shard, 0, 2), swap(shard, 1, 2)
    ahead, behind = jnp.where(one == two, up2, dn2), jnp.where(one == two, dn2, up2)
    up3, dn3 = swap(behind, 0, 1), swap(ahead, 1, 1)
    return shard, up1, dn1, up2, dn2, dn3, up3, swap(dn2, 0, 2)


def scatter_y(own, up1, dn1, up2, dn2, dn3, up3, far):
    one, two = sides()
    far = swap(far, 0, 2)
    behind, ahead = swap(up3, 0, 1), swap(dn3, 1, 1)
    up2 = add(up2, jnp.where(one == two, ahead, behind))
    dn2 = add(dn2, jnp.where(one == two, behind, ahead), far)
    parts = swap(up1, 0, 1), swap(dn1, 1, 1), swap(up2, 0, 2), swap(dn2, 1, 2)
    (out,) = call(last_kernel, (own, *parts), [((LANES, WIDTH), BF16)])
    return out


def y_sums(part):
    return lax.all_to_all(part, "y", 0, 0)


def group_sums(part):
    return lax.all_to_all(part, ("x", "z", "core"), 0, 0)


def on_device(embeddings, prototypes):
    mine = embeddings.transpose(1, 0, 2)
    as_given = Layout(major_to_minor=(0, 1, 2))
    theirs = shift(with_layout_constraint(embeddings, as_given), "core", CORES, 1)
    theirs = with_layout_constraint(theirs, as_given).transpose(1, 0, 2)
    pieces = gather_y(prototypes)
    rows, flat = call(
        rows_kernel,
        (mine, theirs),
        [((VIEWS, ROWS, WIDTH), BF16), ((WIDTH, VIEWS * ROWS), BF16)],
    )
    cols, rows8, rows16 = ((16, LANES), F32), ((8, LANES), F32), ((16, LANES), F32)
    col_out = ((YS, 16, LANES), F32)
    row_out = ((GROUP, 8, LANES), F32)
    both_out = ((GROUP, 16, LANES), BF16)
    work = 4 * ROWS * WIDTH
    early, col_part, soft, near_centers = call(
        early_kernel, (rows, *pieces[:EARLY]),
        [((VIEWS, ROWS, SPLIT), F32), cols, rows8, ((SPLIT, WIDTH), BF16)], (), work * SPLIT,
    )
    late, col_part, soft, far_centers = call(
        late_kernel, (rows, *pieces[EARLY:], col_part, soft),
        [((VIEWS, ROWS, COLS - SPLIT), F32), col_out, rows8, ((COLS - SPLIT, WIDTH), BF16)],
        [cols, rows8], work * (COLS - SPLIT),
    )
    col_part = y_sums(col_part)
    (row_part,) = call(
        functools.partial(row_kernel, True), (early, late, col_part, soft), [both_out],
        [cols, rows8],
    )
    row_part = group_sums(row_part)
    col_part, soft = call(
        functools.partial(col_kernel, True), (early, late, row_part), [col_out, rows8],
        [rows16, cols],
    )
    col_part = y_sums(col_part)
    (row_part,) = call(
        functools.partial(row_kernel, False), (early, late, col_part), [row_out], [cols, rows8]
    )
    row_part = group_sums(row_part)
    (col_part,) = call(
        functools.partial(col_kernel, False), (early, late, row_part), [col_out], [rows8, cols]
    )
    col_part = y_sums(col_part)
    (row_part,) = call(
        functools.partial(row_kernel, False), (early, late, col_part), [row_out], [cols, rows8]
    )
    row_part = group_sums(row_part)

    ge_out = ((XS * ZS, 16, WIDTH), BF16)
    mine, other, grads = call(
        grad_kernel,
        (early, late, row_part, col_part, soft, near_centers, far_centers),
        [ge_out, ge_out, ((VIEWS * ROWS, COLS), BF16)], [cols, rows8], work * COLS,
    )
    sums = call(
        proto_kernel, (flat, grads), [((WIDTH, LANES), BF16)] * SLOTS, (), work * COLS
    )
    theirs = shift(other, "core", CORES, 1)
    mine, sums = lax.optimization_barrier((mine, sums))
    part = add(mine, theirs)
    part = lax.all_to_all(part, ("x", "z"), 0, 0)
    part = jnp.sum(part.astype(F32), axis=0).astype(BF16)
    grad_embed = part.reshape(2, 8, WIDTH).transpose(1, 0, 2)
    own, grad_embed = lax.optimization_barrier((sums[0], grad_embed))
    return grad_embed, scatter_y(own, *sums[1:])


def solution(mesh):
    split = Mesh(mesh.devices.reshape(YS, CORES, XS, ZS), ("y", "core", "x", "z"))
    batch, every = ("y", "core"), ("y", "core", "x", "z")
    return jax.shard_map(
        on_device,
        mesh=split,
        in_specs=(P(batch, None, None), P(every, None)),
        out_specs=(P(every, None, None), P(every, None)),
        check_vma=False,
    )
```

```python
import functools

import jax
import jax.numpy as jnp
from jax import lax
from jax.experimental import pallas as pl
from jax.experimental.layout import Layout, with_layout_constraint
from jax.experimental.pallas import tpu as pltpu
from jax.sharding import Mesh, PartitionSpec as P

PROTOS = 65536
CLIPS = 4096
YS, CORES, XS, ZS = 8, 2, 4, 8
SCALE = 16.0 / 0.1
F32, BF16 = jnp.float32, jnp.bfloat16
LANES = 128
WIDTH = 768
SLOTS = 8
EARLY = 6
MINE = 256
ROWS = CORES * MINE
SPLIT = EARLY * LANES
COLS = SLOTS * LANES
GROUP = XS * ZS
VIEWS = 2
BLOCKS = [(view, half) for view in range(VIEWS) for half in range(CORES)]


def call(kernel, ins, outs, scratch=(), flops=4 * ROWS * COLS):
    return pl.pallas_call(
        kernel,
        out_shape=[jax.ShapeDtypeStruct(shape, dtype) for shape, dtype in outs],
        in_specs=[pl.BlockSpec(memory_space=pltpu.VMEM)] * len(ins),
        out_specs=[pl.BlockSpec(memory_space=pltpu.VMEM)] * len(outs),
        scratch_shapes=[pltpu.VMEM(shape, dtype) for shape, dtype in scratch],
        compiler_params=pltpu.CompilerParams(vmem_limit_bytes=16 * 1024 * 1024),
        cost_estimate=pl.CostEstimate(flops=flops, bytes_accessed=2 << 20, transcendentals=0),
    )(*ins)


def sides():
    y, core = lax.axis_index("y"), lax.axis_index("core")
    return 1 - 2 * lax.rem(y + core, 2), 1 - 2 * lax.rem(y // 2 + core, 2)


def places():
    y, (one, two) = lax.axis_index("y"), sides()
    steps = (0, one, -one, 2 * two, -2 * two, -3 * one, 3 * one, 4)
    return [lax.axis_index("core")] + [lax.rem(y + step + YS, YS) for step in steps]


def turned(block):
    return jnp.sum(block.T, axis=0, keepdims=True)


def down(row):
    return jnp.broadcast_to(row, (LANES, LANES)).T


def lanes_of(slot):
    return slice(slot * LANES, (slot + 1) * LANES)


def clips_of(half):
    return slice(half * MINE, (half + 1) * MINE)


def clip_row(s, view, half, part):
    return view * 4 + jnp.bitwise_xor(s[0], half) * 2 + part


def put_clips(s, view, half, acc, out):
    for part in range(2):
        block = acc[part * LANES : (part + 1) * LANES]
        out[pl.ds(clip_row(s, view, half, part), 1), :] = turned(block)


def clip_scale(s, view, half, ref, scale):
    rows = [ref[pl.ds(clip_row(s, view, half, part), 1), :] for part in range(2)]
    return jnp.concatenate([down(scale / row) for row in rows])


def put_cols(s, view, slot, value, out):
    out[pl.ds(view * YS + s[1 + slot], 1), :] = value


def col_scale(s, view, slot, ref):
    return 1.0 / (PROTOS * ref[pl.ds(view * YS + s[1 + slot], 1), :])


def copies(ref, value):
    ref[...] = jnp.broadcast_to(value.astype(ref.dtype)[None], ref.shape)


def units(values):
    wide = values.astype(F32)
    norm = lax.rsqrt(jnp.sum(wide * wide, axis=-1, keepdims=True) + 1e-06)
    return (wide * norm).astype(BF16)


def rows_kernel(mine_ref, theirs_ref, rows_ref, flat_ref):
    for half, ref in enumerate((mine_ref, theirs_ref)):
        for view in range(VIEWS):
            unit = units(ref[view])
            rows_ref[view, clips_of(half)] = unit
            start = (half * VIEWS + view) * MINE
            flat_ref[:, start : start + MINE] = unit.T


def score(s, slots, rows, pieces, e_ref, centers, part, soft):
    for place, piece in enumerate(pieces):
        centers[lanes_of(place)] = units(piece[...])
    for view in range(VIEWS):
        acc = None
        for chunk in range(0, len(slots), 2):
            lanes = slice(chunk * LANES, (chunk + 2) * LANES)
            scores = lax.dot_general(
                rows[view], centers[lanes], (((1,), (1,)), ((), ())), preferred_element_type=F32
            )
            likely = jnp.exp(scores * 10.0)
            e_ref[view, :, lanes] = likely
            sums = jnp.sum(likely * likely, axis=0, keepdims=True)
            put_cols(s, view, slots[chunk], sums[:, :LANES], part)
            put_cols(s, view, slots[chunk + 1], sums[:, LANES:], part)
            both = likely[:, :LANES] + likely[:, LANES:]
            acc = both if acc is None else acc + both
        for half in range(CORES):
            put_clips(s, view, half, acc[clips_of(half)], soft)


def early_kernel(rows, *refs):
    s = places()
    pieces, (e_ref, part, soft, centers) = refs[:EARLY], refs[EARLY:]
    part[...] = jnp.zeros_like(part)
    score(s, range(EARLY), rows, pieces, e_ref, centers, part, soft)


def late_kernel(rows, *refs):
    s = places()
    late = SLOTS - EARLY
    pieces, (early_part, early_soft, e_ref, cols_ref, soft_ref, centers, part, soft) = (
        refs[:late],
        refs[late:],
    )
    part[...] = jnp.zeros_like(part)
    score(s, range(EARLY, SLOTS), rows, pieces, e_ref, centers, part, soft)
    soft_ref[...] = early_soft[...] + soft[...]
    copies(cols_ref, early_part[...] + part[...])


def likely_of(e_refs, view, rows, slot):
    early, late = e_refs
    return early[view, rows, lanes_of(slot)] if slot < EARLY else late[view, rows, lanes_of(slot - EARLY)]


def row_kernel(first, early, late, recv_ref, *refs):
    s = places()
    if first:
        soft_ref, out_ref, total, sums = refs
    else:
        out_ref, total, sums = refs
    total[...] = jnp.sum(recv_ref[...].astype(F32), axis=0)
    for view, half in BLOCKS:
        acc = None
        for slot in range(SLOTS):
            likely = likely_of((early, late), view, clips_of(half), slot)
            term = likely * likely * col_scale(s, view, slot, total)
            acc = term if acc is None else acc + term
        put_clips(s, view, half, acc, sums)
    both = sums[...]
    if first:
        both = jnp.concatenate([both, soft_ref[...]])
    out_ref[...] = both


def col_kernel(first, early, late, recv_ref, *refs):
    s = places()
    if first:
        out_ref, soft_ref, total, sums = refs
    else:
        out_ref, total, sums = refs
    total[...] = jnp.sum(recv_ref[...].astype(F32), axis=0)
    if first:
        soft_ref[...] = total[8:]
    for view in range(VIEWS):
        scale = [clip_scale(s, view, half, total, 1.0 / CLIPS) for half in range(CORES)]
        scale = jnp.concatenate(scale)
        for slot in range(SLOTS):
            likely = likely_of((early, late), view, slice(None), slot)
            value = jnp.sum(likely * likely * scale, axis=0, keepdims=True)
            put_cols(s, view, slot, value, sums)
    copies(out_ref, sums[...])


def grad_kernel(
    early, late, row_ref, col_ref, soft_ref, near_centers, far_centers,
    mine_ref, other_ref, grads, total, clips,
):
    s = places()
    total[...] = jnp.sum(col_ref[...].astype(F32), axis=0)
    clips[...] = jnp.sum(row_ref[...], axis=0)
    for half, ref in ((1, other_ref), (0, mine_ref)):
        rows = clips_of(half)
        code = [clip_scale(s, view, half, clips, SCALE) for view in range(VIEWS)]
        start = half * VIEWS * MINE
        for view in range(VIEWS):
            soft = clip_scale(s, view, half, soft_ref, SCALE)
            for slot in range(SLOTS):
                likely = likely_of((early, late), view, rows, slot)
                swapped = likely_of((early, late), 1 - view, rows, slot)
                scale = col_scale(s, 1 - view, slot, total)
                value = likely * soft - swapped * swapped * code[1 - view] * scale
                place = start + view * MINE
                grads[place : place + MINE, lanes_of(slot)] = value.astype(BF16)
        part = slice(start, start + VIEWS * MINE)
        out = jnp.dot(grads[part, :SPLIT], near_centers[...], preferred_element_type=F32)
        out = out + jnp.dot(grads[part, SPLIT:], far_centers[...], preferred_element_type=F32)
        for place in range(XS * ZS):
            eight = [out[view * MINE + place * 8 : view * MINE + place * 8 + 8] for view in range(2)]
            ref[place] = jnp.concatenate(eight).astype(BF16)


def proto_kernel(flat_ref, grads, *outs):
    for chunk in range(0, SLOTS, 2):
        lanes = slice(chunk * LANES, (chunk + 2) * LANES)
        out = jnp.dot(flat_ref[...], grads[:, lanes], preferred_element_type=F32).astype(BF16)
        outs[chunk][...] = out[:, :LANES]
        outs[chunk + 1][...] = out[:, LANES:]


def last_kernel(own, *refs):
    *parts, out_ref = refs
    total = own[...].astype(F32)
    for part in parts:
        total = total + part[...].astype(F32)
    out_ref[...] = total.T.astype(BF16)


def shift(part, axis, size, by):
    return lax.ppermute(part, axis, [(i, (i + by) % size) for i in range(size)])


def add(*parts):
    total = parts[0].astype(F32)
    for part in parts[1:]:
        total = total + part.astype(F32)
    return total.astype(BF16)


def swap(part, side, by):
    pairs = []
    for core in range(CORES):
        for y in range(YS):
            if (y // by) % 2 == (side + core) % 2:
                one, two = y * CORES + core, (y + by) % YS * CORES + core
                pairs += [(one, two), (two, one)]
    return lax.ppermute(part, ("y", "core"), pairs)


def gather_y(shard):
    one, two = sides()
    up1, dn1 = swap(shard, 0, 1), swap(shard, 1, 1)
    up2, dn2 = swap(shard, 0, 2), swap(shard, 1, 2)
    ahead, behind = jnp.where(one == two, up2, dn2), jnp.where(one == two, dn2, up2)
    up3, dn3 = swap(behind, 0, 1), swap(ahead, 1, 1)
    return shard, up1, dn1, up2, dn2, dn3, up3, swap(dn2, 0, 2)


def scatter_y(own, up1, dn1, up2, dn2, dn3, up3, far):
    one, two = sides()
    far = swap(far, 0, 2)
    behind, ahead = swap(up3, 0, 1), swap(dn3, 1, 1)
    up2 = add(up2, jnp.where(one == two, ahead, behind))
    dn2 = add(dn2, jnp.where(one == two, behind, ahead), far)
    parts = swap(up1, 0, 1), swap(dn1, 1, 1), swap(up2, 0, 2), swap(dn2, 1, 2)
    (out,) = call(last_kernel, (own, *parts), [((LANES, WIDTH), BF16)])
    return out


def y_sums(part):
    return lax.all_to_all(part, "y", 0, 0)


def group_sums(part, dtype):
    part = (part + shift(part, "core", CORES, 1)).astype(dtype)
    part = jnp.broadcast_to(part[None], (GROUP,) + part.shape)
    return lax.all_to_all(part, ("z", "x"), 0, 0)


def on_device(embeddings, prototypes):
    mine = embeddings.transpose(1, 0, 2)
    as_given = Layout(major_to_minor=(0, 1, 2))
    theirs = shift(with_layout_constraint(embeddings, as_given), "core", CORES, 1)
    theirs = with_layout_constraint(theirs, as_given).transpose(1, 0, 2)
    pieces = gather_y(prototypes)
    rows, flat = call(
        rows_kernel,
        (mine, theirs),
        [((VIEWS, ROWS, WIDTH), BF16), ((WIDTH, VIEWS * ROWS), BF16)],
    )
    cols, rows8, rows16 = ((16, LANES), F32), ((8, LANES), F32), ((16, LANES), F32)
    col_out = ((YS, 16, LANES), BF16)
    row_out = ((8, LANES), F32)
    both_out = ((16, LANES), F32)
    work = 4 * ROWS * WIDTH
    early, col_part, soft, near_centers = call(
        early_kernel, (rows, *pieces[:EARLY]),
        [((VIEWS, ROWS, SPLIT), F32), cols, rows8, ((SPLIT, WIDTH), BF16)], (), work * SPLIT,
    )
    late, col_part, soft, far_centers = call(
        late_kernel, (rows, *pieces[EARLY:], col_part, soft),
        [((VIEWS, ROWS, COLS - SPLIT), F32), col_out, rows8, ((COLS - SPLIT, WIDTH), BF16)],
        [cols, rows8], work * (COLS - SPLIT),
    )
    col_part = y_sums(col_part)
    (row_part,) = call(
        functools.partial(row_kernel, True), (early, late, col_part, soft), [both_out],
        [cols, rows8],
    )
    row_part = group_sums(row_part, BF16)
    col_part, soft = call(
        functools.partial(col_kernel, True), (early, late, row_part), [col_out, rows8],
        [rows16, cols],
    )
    col_part = y_sums(col_part)
    (row_part,) = call(
        functools.partial(row_kernel, False), (early, late, col_part), [row_out], [cols, rows8]
    )
    row_part = group_sums(row_part, F32)
    (col_part,) = call(
        functools.partial(col_kernel, False), (early, late, row_part), [col_out], [rows8, cols]
    )
    col_part = y_sums(col_part)
    (row_part,) = call(
        functools.partial(row_kernel, False), (early, late, col_part), [row_out], [cols, rows8]
    )
    row_part = group_sums(row_part, F32)

    ge_out = ((XS * ZS, 16, WIDTH), BF16)
    mine, other, grads = call(
        grad_kernel,
        (early, late, row_part, col_part, soft, near_centers, far_centers),
        [ge_out, ge_out, ((VIEWS * ROWS, COLS), BF16)], [cols, rows8], work * COLS,
    )
    sums = call(
        proto_kernel, (flat, grads), [((WIDTH, LANES), BF16)] * SLOTS, (), work * COLS
    )
    theirs = shift(other, "core", CORES, 1)
    mine, sums = lax.optimization_barrier((mine, sums))
    part = add(mine, theirs)
    part = lax.all_to_all(part, ("x", "z"), 0, 0)
    part = jnp.sum(part.astype(F32), axis=0).astype(BF16)
    grad_embed = part.reshape(2, 8, WIDTH).transpose(1, 0, 2)
    own, grad_embed = lax.optimization_barrier((sums[0], grad_embed))
    return grad_embed, scatter_y(own, *sums[1:])


def solution(mesh):
    split = Mesh(mesh.devices.reshape(YS, CORES, XS, ZS), ("y", "core", "x", "z"))
    batch, every = ("y", "core"), ("y", "core", "x", "z")
    return jax.shard_map(
        on_device,
        mesh=split,
        in_specs=(P(batch, None, None), P(every, None)),
        out_specs=(P(every, None, None), P(every, None)),
        check_vma=False,
    )
```

```python
import functools

import jax
import jax.numpy as jnp
from jax import lax
from jax.experimental import pallas as pl
from jax.experimental.layout import Layout, with_layout_constraint
from jax.experimental.pallas import tpu as pltpu
from jax.sharding import Mesh, PartitionSpec as P

PROTOS = 65536
CLIPS = 4096
YS, CORES, XS, ZS = 8, 2, 4, 8
SCALE = 16.0 / 0.1
F32, BF16 = jnp.float32, jnp.bfloat16
LANES = 128
WIDTH = 768
SLOTS = 8
EARLY = 6
MINE = 256
ROWS = CORES * MINE
SPLIT = EARLY * LANES
COLS = SLOTS * LANES
GROUP = XS * ZS
VIEWS = 2
BLOCKS = [(view, half) for view in range(VIEWS) for half in range(CORES)]


def call(kernel, ins, outs, scratch=(), flops=4 * ROWS * COLS):
    return pl.pallas_call(
        kernel,
        out_shape=[jax.ShapeDtypeStruct(shape, dtype) for shape, dtype in outs],
        in_specs=[pl.BlockSpec(memory_space=pltpu.VMEM)] * len(ins),
        out_specs=[pl.BlockSpec(memory_space=pltpu.VMEM)] * len(outs),
        scratch_shapes=[pltpu.VMEM(shape, dtype) for shape, dtype in scratch],
        compiler_params=pltpu.CompilerParams(vmem_limit_bytes=16 * 1024 * 1024),
        cost_estimate=pl.CostEstimate(flops=flops, bytes_accessed=2 << 20, transcendentals=0),
    )(*ins)


def sides():
    y, core = lax.axis_index("y"), lax.axis_index("core")
    return 1 - 2 * lax.rem(y + core, 2), 1 - 2 * lax.rem(y // 2 + core, 2)


def places():
    y, (one, two) = lax.axis_index("y"), sides()
    steps = (0, one, -one, 2 * two, -2 * two, -3 * one, 3 * one, 4)
    return [lax.axis_index("core")] + [lax.rem(y + step + YS, YS) for step in steps]


def turned(block):
    return jnp.sum(block.T, axis=0, keepdims=True)


def down(row):
    return jnp.broadcast_to(row, (LANES, LANES)).T


def lanes_of(slot):
    return slice(slot * LANES, (slot + 1) * LANES)


def clips_of(half):
    return slice(half * MINE, (half + 1) * MINE)


def clip_row(s, view, half, part):
    return view * 4 + jnp.bitwise_xor(s[0], half) * 2 + part


def put_clips(s, view, half, acc, out):
    for part in range(2):
        block = acc[part * LANES : (part + 1) * LANES]
        out[pl.ds(clip_row(s, view, half, part), 1), :] = turned(block)


def clip_scale(s, view, half, ref, scale):
    rows = [ref[pl.ds(clip_row(s, view, half, part), 1), :] for part in range(2)]
    return jnp.concatenate([down(scale / row) for row in rows])


def put_cols(s, view, slot, value, out):
    out[pl.ds(view * YS + s[1 + slot], 1), :] = value


def col_scale(s, view, slot, ref):
    return 1.0 / (PROTOS * ref[pl.ds(view * YS + s[1 + slot], 1), :])


def copies(ref, value):
    ref[...] = jnp.broadcast_to(value.astype(ref.dtype)[None], ref.shape)


def units(values):
    wide = values.astype(F32)
    norm = lax.rsqrt(jnp.sum(wide * wide, axis=-1, keepdims=True) + 1e-06)
    return (wide * norm).astype(BF16)


def rows_kernel(mine_ref, theirs_ref, rows_ref, flat_ref):
    for half, ref in enumerate((mine_ref, theirs_ref)):
        for view in range(VIEWS):
            unit = units(ref[view])
            rows_ref[view, clips_of(half)] = unit
            start = (half * VIEWS + view) * MINE
            flat_ref[:, start : start + MINE] = unit.T


def score(s, slots, rows, pieces, e_ref, centers, part, soft):
    for place, piece in enumerate(pieces):
        centers[lanes_of(place)] = units(piece[...])
    for view in range(VIEWS):
        acc = None
        for chunk in range(0, len(slots), 2):
            lanes = slice(chunk * LANES, (chunk + 2) * LANES)
            scores = lax.dot_general(
                rows[view], centers[lanes], (((1,), (1,)), ((), ())), preferred_element_type=F32
            )
            likely = jnp.exp(scores * 10.0)
            e_ref[view, :, lanes] = likely
            sums = jnp.sum(likely * likely, axis=0, keepdims=True)
            put_cols(s, view, slots[chunk], sums[:, :LANES], part)
            put_cols(s, view, slots[chunk + 1], sums[:, LANES:], part)
            both = likely[:, :LANES] + likely[:, LANES:]
            acc = both if acc is None else acc + both
        for half in range(CORES):
            put_clips(s, view, half, acc[clips_of(half)], soft)


def early_kernel(rows, *refs):
    s = places()
    pieces, (e_ref, part, soft, centers) = refs[:EARLY], refs[EARLY:]
    part[...] = jnp.zeros_like(part)
    score(s, range(EARLY), rows, pieces, e_ref, centers, part, soft)


def late_kernel(rows, *refs):
    s = places()
    late = SLOTS - EARLY
    pieces, (early_part, early_soft, e_ref, cols_ref, soft_ref, centers, part, soft) = (
        refs[:late],
        refs[late:],
    )
    part[...] = jnp.zeros_like(part)
    score(s, range(EARLY, SLOTS), rows, pieces, e_ref, centers, part, soft)
    soft_ref[...] = early_soft[...] + soft[...]
    copies(cols_ref, early_part[...] + part[...])


def likely_of(e_refs, view, rows, slot):
    early, late = e_refs
    return early[view, rows, lanes_of(slot)] if slot < EARLY else late[view, rows, lanes_of(slot - EARLY)]


def row_kernel(first, early, late, recv_ref, *refs):
    s = places()
    if first:
        soft_ref, out_ref, total, sums = refs
    else:
        out_ref, total, sums = refs
    total[...] = jnp.sum(recv_ref[...].astype(F32), axis=0)
    for view, half in BLOCKS:
        acc = None
        for slot in range(SLOTS):
            likely = likely_of((early, late), view, clips_of(half), slot)
            term = likely * likely * col_scale(s, view, slot, total)
            acc = term if acc is None else acc + term
        put_clips(s, view, half, acc, sums)
    both = sums[...]
    if first:
        both = jnp.concatenate([both, soft_ref[...]])
    out_ref[...] = both


def col_kernel(first, early, late, recv_ref, *refs):
    s = places()
    if first:
        out_ref, soft_ref, total, sums = refs
    else:
        out_ref, total, sums = refs
    total[...] = jnp.sum(recv_ref[...].astype(F32), axis=0)
    if first:
        soft_ref[...] = total[8:]
    for view in range(VIEWS):
        scale = [clip_scale(s, view, half, total, 1.0 / CLIPS) for half in range(CORES)]
        scale = jnp.concatenate(scale)
        for slot in range(SLOTS):
            likely = likely_of((early, late), view, slice(None), slot)
            value = jnp.sum(likely * likely * scale, axis=0, keepdims=True)
            put_cols(s, view, slot, value, sums)
    copies(out_ref, sums[...])


def grad_kernel(
    early, late, row_ref, col_ref, soft_ref, near_centers, far_centers,
    mine_ref, other_ref, grads, total, clips,
):
    s = places()
    total[...] = jnp.sum(col_ref[...].astype(F32), axis=0)
    clips[...] = jnp.sum(row_ref[...].astype(F32), axis=0)
    for half, ref in ((1, other_ref), (0, mine_ref)):
        rows = clips_of(half)
        code = [clip_scale(s, view, half, clips, SCALE) for view in range(VIEWS)]
        start = half * VIEWS * MINE
        for view in range(VIEWS):
            soft = clip_scale(s, view, half, soft_ref, SCALE)
            for slot in range(SLOTS):
                likely = likely_of((early, late), view, rows, slot)
                swapped = likely_of((early, late), 1 - view, rows, slot)
                scale = col_scale(s, 1 - view, slot, total)
                value = likely * soft - swapped * swapped * code[1 - view] * scale
                place = start + view * MINE
                grads[place : place + MINE, lanes_of(slot)] = value.astype(BF16)
        part = slice(start, start + VIEWS * MINE)
        out = jnp.dot(grads[part, :SPLIT], near_centers[...], preferred_element_type=F32)
        out = out + jnp.dot(grads[part, SPLIT:], far_centers[...], preferred_element_type=F32)
        for place in range(XS * ZS):
            eight = [out[view * MINE + place * 8 : view * MINE + place * 8 + 8] for view in range(2)]
            ref[place] = jnp.concatenate(eight).astype(BF16)


def proto_kernel(flat_ref, grads, *outs):
    for chunk in range(0, SLOTS, 2):
        lanes = slice(chunk * LANES, (chunk + 2) * LANES)
        out = jnp.dot(flat_ref[...], grads[:, lanes], preferred_element_type=F32).astype(BF16)
        outs[chunk][...] = out[:, :LANES]
        outs[chunk + 1][...] = out[:, LANES:]


def last_kernel(own, *refs):
    *parts, out_ref = refs
    total = own[...].astype(F32)
    for part in parts:
        total = total + part[...].astype(F32)
    out_ref[...] = total.T.astype(BF16)


def shift(part, axis, size, by):
    return lax.ppermute(part, axis, [(i, (i + by) % size) for i in range(size)])


def add(*parts):
    total = parts[0].astype(F32)
    for part in parts[1:]:
        total = total + part.astype(F32)
    return total.astype(BF16)


def swap(part, side, by):
    pairs = []
    for core in range(CORES):
        for y in range(YS):
            if (y // by) % 2 == (side + core) % 2:
                one, two = y * CORES + core, (y + by) % YS * CORES + core
                pairs += [(one, two), (two, one)]
    return lax.ppermute(part, ("y", "core"), pairs)


def gather_y(shard):
    one, two = sides()
    up1, dn1 = swap(shard, 0, 1), swap(shard, 1, 1)
    up2, dn2 = swap(shard, 0, 2), swap(shard, 1, 2)
    ahead, behind = jnp.where(one == two, up2, dn2), jnp.where(one == two, dn2, up2)
    up3, dn3 = swap(behind, 0, 1), swap(ahead, 1, 1)
    return shard, up1, dn1, up2, dn2, dn3, up3, swap(dn2, 0, 2)


def scatter_y(own, up1, dn1, up2, dn2, dn3, up3, far):
    one, two = sides()
    far = swap(far, 0, 2)
    behind, ahead = swap(up3, 0, 1), swap(dn3, 1, 1)
    up2 = add(up2, jnp.where(one == two, ahead, behind))
    dn2 = add(dn2, jnp.where(one == two, behind, ahead), far)
    parts = swap(up1, 0, 1), swap(dn1, 1, 1), swap(up2, 0, 2), swap(dn2, 1, 2)
    (out,) = call(last_kernel, (own, *parts), [((LANES, WIDTH), BF16)])
    return out


def y_sums(part):
    return lax.all_to_all(part, "y", 0, 0)


def group_sums(part, dtype):
    part = (part + shift(part, "core", CORES, 1)).astype(dtype)
    part = jnp.broadcast_to(part[None], (GROUP,) + part.shape)
    return lax.all_to_all(part, ("z", "x"), 0, 0)


def on_device(embeddings, prototypes):
    mine = embeddings.transpose(1, 0, 2)
    as_given = Layout(major_to_minor=(0, 1, 2))
    theirs = shift(with_layout_constraint(embeddings, as_given), "core", CORES, 1)
    theirs = with_layout_constraint(theirs, as_given).transpose(1, 0, 2)
    pieces = gather_y(prototypes)
    rows, flat = call(
        rows_kernel,
        (mine, theirs),
        [((VIEWS, ROWS, WIDTH), BF16), ((WIDTH, VIEWS * ROWS), BF16)],
    )
    cols, rows8, rows16 = ((16, LANES), F32), ((8, LANES), F32), ((16, LANES), F32)
    col_out = ((YS, 16, LANES), BF16)
    row_out = ((8, LANES), F32)
    both_out = ((16, LANES), F32)
    work = 4 * ROWS * WIDTH
    early, col_part, soft, near_centers = call(
        early_kernel, (rows, *pieces[:EARLY]),
        [((VIEWS, ROWS, SPLIT), F32), cols, rows8, ((SPLIT, WIDTH), BF16)], (), work * SPLIT,
    )
    late, col_part, soft, far_centers = call(
        late_kernel, (rows, *pieces[EARLY:], col_part, soft),
        [((VIEWS, ROWS, COLS - SPLIT), F32), col_out, rows8, ((COLS - SPLIT, WIDTH), BF16)],
        [cols, rows8], work * (COLS - SPLIT),
    )
    col_part = y_sums(col_part)
    (row_part,) = call(
        functools.partial(row_kernel, True), (early, late, col_part, soft), [both_out],
        [cols, rows8],
    )
    row_part = group_sums(row_part, BF16)
    col_part, soft = call(
        functools.partial(col_kernel, True), (early, late, row_part), [col_out, rows8],
        [rows16, cols],
    )
    col_part = y_sums(col_part)
    (row_part,) = call(
        functools.partial(row_kernel, False), (early, late, col_part), [row_out], [cols, rows8]
    )
    row_part = group_sums(row_part, BF16)
    (col_part,) = call(
        functools.partial(col_kernel, False), (early, late, row_part), [col_out], [rows8, cols]
    )
    col_part = y_sums(col_part)
    (row_part,) = call(
        functools.partial(row_kernel, False), (early, late, col_part), [row_out], [cols, rows8]
    )
    row_part = group_sums(row_part, BF16)

    ge_out = ((XS * ZS, 16, WIDTH), BF16)
    mine, other, grads = call(
        grad_kernel,
        (early, late, row_part, col_part, soft, near_centers, far_centers),
        [ge_out, ge_out, ((VIEWS * ROWS, COLS), BF16)], [cols, rows8], work * COLS,
    )
    sums = call(
        proto_kernel, (flat, grads), [((WIDTH, LANES), BF16)] * SLOTS, (), work * COLS
    )
    theirs = shift(other, "core", CORES, 1)
    mine, sums = lax.optimization_barrier((mine, sums))
    part = add(mine, theirs)
    part = lax.all_to_all(part, ("x", "z"), 0, 0)
    part = jnp.sum(part.astype(F32), axis=0).astype(BF16)
    grad_embed = part.reshape(2, 8, WIDTH).transpose(1, 0, 2)
    own, grad_embed = lax.optimization_barrier((sums[0], grad_embed))
    return grad_embed, scatter_y(own, *sums[1:])


def solution(mesh):
    split = Mesh(mesh.devices.reshape(YS, CORES, XS, ZS), ("y", "core", "x", "z"))
    batch, every = ("y", "core"), ("y", "core", "x", "z")
    return jax.shard_map(
        on_device,
        mesh=split,
        in_specs=(P(batch, None, None), P(every, None)),
        out_specs=(P(every, None, None), P(every, None)),
        check_vma=False,
    )
```

```python
import functools

import jax
import jax.numpy as jnp
from jax import lax
from jax.experimental import pallas as pl
from jax.experimental.layout import Layout, with_layout_constraint
from jax.experimental.pallas import tpu as pltpu
from jax.sharding import Mesh, PartitionSpec as P

PROTOS = 65536
CLIPS = 4096
YS, CORES, XS, ZS = 8, 2, 4, 8
SCALE = 16.0 / 0.1
F32, BF16 = jnp.float32, jnp.bfloat16
LANES = 128
WIDTH = 768
SLOTS = 8
EARLY = 6
MINE = 256
ROWS = CORES * MINE
SPLIT = EARLY * LANES
COLS = SLOTS * LANES
GROUP = XS * ZS
VIEWS = 2
BLOCKS = [(view, half) for view in range(VIEWS) for half in range(CORES)]


def call(kernel, ins, outs, scratch=(), flops=4 * ROWS * COLS):
    return pl.pallas_call(
        kernel,
        out_shape=[jax.ShapeDtypeStruct(shape, dtype) for shape, dtype in outs],
        in_specs=[pl.BlockSpec(memory_space=pltpu.VMEM)] * len(ins),
        out_specs=[pl.BlockSpec(memory_space=pltpu.VMEM)] * len(outs),
        scratch_shapes=[pltpu.VMEM(shape, dtype) for shape, dtype in scratch],
        compiler_params=pltpu.CompilerParams(vmem_limit_bytes=16 * 1024 * 1024),
        cost_estimate=pl.CostEstimate(flops=flops, bytes_accessed=2 << 20, transcendentals=0),
    )(*ins)


def sides():
    y, core = lax.axis_index("y"), lax.axis_index("core")
    return 1 - 2 * lax.rem(y + core, 2), 1 - 2 * lax.rem(y // 2 + core, 2)


def places():
    y, (one, two) = lax.axis_index("y"), sides()
    steps = (0, one, -one, 2 * two, -2 * two, -3 * one, 3 * one, 4)
    return [lax.axis_index("core")] + [lax.rem(y + step + YS, YS) for step in steps]


def turned(block):
    return jnp.sum(block.T, axis=0, keepdims=True)


def down(row):
    return jnp.broadcast_to(row, (LANES, LANES)).T


def lanes_of(slot):
    return slice(slot * LANES, (slot + 1) * LANES)


def clips_of(half):
    return slice(half * MINE, (half + 1) * MINE)


def clip_row(s, view, half, part):
    return view * 4 + jnp.bitwise_xor(s[0], half) * 2 + part


def put_clips(s, view, half, acc, out):
    for part in range(2):
        block = acc[part * LANES : (part + 1) * LANES]
        out[pl.ds(clip_row(s, view, half, part), 1), :] = turned(block)


def clip_scale(s, view, half, ref, scale):
    rows = [ref[pl.ds(clip_row(s, view, half, part), 1), :] for part in range(2)]
    return jnp.concatenate([down(scale / row) for row in rows])


def put_cols(s, view, slot, value, out):
    out[pl.ds(view * YS + s[1 + slot], 1), :] = value


def col_scale(s, view, slot, ref):
    return 1.0 / (PROTOS * ref[pl.ds(view * YS + s[1 + slot], 1), :])


def copies(ref, value):
    ref[...] = jnp.broadcast_to(value.astype(ref.dtype)[None], ref.shape)


def units(values):
    wide = values.astype(F32)
    norm = lax.rsqrt(jnp.sum(wide * wide, axis=-1, keepdims=True) + 1e-06)
    return (wide * norm).astype(BF16)


def rows_kernel(mine_ref, theirs_ref, rows_ref, flat_ref):
    for half, ref in enumerate((mine_ref, theirs_ref)):
        for view in range(VIEWS):
            unit = units(ref[view])
            rows_ref[view, clips_of(half)] = unit
            start = (half * VIEWS + view) * MINE
            flat_ref[:, start : start + MINE] = unit.T


def score(s, slots, rows, pieces, e_ref, centers, part, soft):
    for place, piece in enumerate(pieces):
        centers[lanes_of(place)] = units(piece[...])
    for view in range(VIEWS):
        acc = None
        for chunk in range(0, len(slots), 2):
            lanes = slice(chunk * LANES, (chunk + 2) * LANES)
            scores = lax.dot_general(
                rows[view], centers[lanes], (((1,), (1,)), ((), ())), preferred_element_type=F32
            )
            likely = jnp.exp(scores * 10.0)
            e_ref[view, :, lanes] = likely
            sums = jnp.sum(likely * likely, axis=0, keepdims=True)
            put_cols(s, view, slots[chunk], sums[:, :LANES], part)
            put_cols(s, view, slots[chunk + 1], sums[:, LANES:], part)
            both = likely[:, :LANES] + likely[:, LANES:]
            acc = both if acc is None else acc + both
        for half in range(CORES):
            put_clips(s, view, half, acc[clips_of(half)], soft)


def early_kernel(rows, *refs):
    s = places()
    pieces, (e_ref, part, soft, centers) = refs[:EARLY], refs[EARLY:]
    part[...] = jnp.zeros_like(part)
    score(s, range(EARLY), rows, pieces, e_ref, centers, part, soft)


def late_kernel(rows, *refs):
    s = places()
    late = SLOTS - EARLY
    pieces, (early_part, early_soft, e_ref, cols_ref, soft_ref, centers, part, soft) = (
        refs[:late],
        refs[late:],
    )
    part[...] = jnp.zeros_like(part)
    score(s, range(EARLY, SLOTS), rows, pieces, e_ref, centers, part, soft)
    soft_ref[...] = early_soft[...] + soft[...]
    copies(cols_ref, early_part[...] + part[...])


def likely_of(e_refs, view, rows, slot):
    early, late = e_refs
    return early[view, rows, lanes_of(slot)] if slot < EARLY else late[view, rows, lanes_of(slot - EARLY)]


def row_kernel(first, early, late, recv_ref, *refs):
    s = places()
    if first:
        soft_ref, out_ref, total, sums = refs
    else:
        out_ref, total, sums = refs
    total[...] = jnp.sum(recv_ref[...].astype(F32), axis=0)
    for view, half in BLOCKS:
        acc = None
        for slot in range(SLOTS):
            likely = likely_of((early, late), view, clips_of(half), slot)
            term = likely * likely * col_scale(s, view, slot, total)
            acc = term if acc is None else acc + term
        put_clips(s, view, half, acc, sums)
    both = sums[...]
    if first:
        both = jnp.concatenate([both, soft_ref[...]])
    out_ref[...] = both


def col_kernel(first, early, late, recv_ref, *refs):
    s = places()
    if first:
        out_ref, soft_ref, total, sums = refs
    else:
        out_ref, total, sums = refs
    total[...] = jnp.sum(recv_ref[...].astype(F32), axis=0)
    if first:
        soft_ref[...] = total[8:]
    for view in range(VIEWS):
        scale = [clip_scale(s, view, half, total, 1.0 / CLIPS) for half in range(CORES)]
        scale = jnp.concatenate(scale)
        for slot in range(SLOTS):
            likely = likely_of((early, late), view, slice(None), slot)
            value = jnp.sum(likely * likely * scale, axis=0, keepdims=True)
            put_cols(s, view, slot, value, sums)
    copies(out_ref, sums[...])


def grad_kernel(
    early, late, row_ref, col_ref, soft_ref, near_centers, far_centers,
    mine_ref, other_ref, grads, total, clips,
):
    s = places()
    total[...] = jnp.sum(col_ref[...].astype(F32), axis=0)
    clips[...] = jnp.sum(row_ref[...].astype(F32), axis=0)
    for half, ref in ((1, other_ref), (0, mine_ref)):
        rows = clips_of(half)
        code = [clip_scale(s, view, half, clips, SCALE) for view in range(VIEWS)]
        start = half * VIEWS * MINE
        for view in range(VIEWS):
            soft = clip_scale(s, view, half, soft_ref, SCALE)
            for slot in range(SLOTS):
                likely = likely_of((early, late), view, rows, slot)
                swapped = likely_of((early, late), 1 - view, rows, slot)
                scale = col_scale(s, 1 - view, slot, total)
                value = likely * soft - swapped * swapped * code[1 - view] * scale
                place = start + view * MINE
                grads[place : place + MINE, lanes_of(slot)] = value.astype(BF16)
        part = slice(start, start + VIEWS * MINE)
        out = jnp.dot(grads[part, :SPLIT], near_centers[...], preferred_element_type=F32)
        out = out + jnp.dot(grads[part, SPLIT:], far_centers[...], preferred_element_type=F32)
        for place in range(XS * ZS):
            eight = [out[view * MINE + place * 8 : view * MINE + place * 8 + 8] for view in range(2)]
            ref[place % ZS * XS + place // ZS] = jnp.concatenate(eight).astype(BF16)


def proto_kernel(flat_ref, grads, *outs):
    for chunk in range(0, SLOTS, 2):
        lanes = slice(chunk * LANES, (chunk + 2) * LANES)
        out = jnp.dot(flat_ref[...], grads[:, lanes], preferred_element_type=F32).astype(BF16)
        outs[chunk][...] = out[:, :LANES]
        outs[chunk + 1][...] = out[:, LANES:]


def last_kernel(own, *refs):
    *parts, out_ref = refs
    total = own[...].astype(F32)
    for part in parts:
        total = total + part[...].astype(F32)
    out_ref[...] = total.T.astype(BF16)


def shift(part, axis, size, by):
    return lax.ppermute(part, axis, [(i, (i + by) % size) for i in range(size)])


def add(*parts):
    total = parts[0].astype(F32)
    for part in parts[1:]:
        total = total + part.astype(F32)
    return total.astype(BF16)


def swap(part, side, by):
    pairs = []
    for core in range(CORES):
        for y in range(YS):
            if (y // by) % 2 == (side + core) % 2:
                one, two = y * CORES + core, (y + by) % YS * CORES + core
                pairs += [(one, two), (two, one)]
    return lax.ppermute(part, ("y", "core"), pairs)


def gather_y(shard):
    one, two = sides()
    up1, dn1 = swap(shard, 0, 1), swap(shard, 1, 1)
    up2, dn2 = swap(shard, 0, 2), swap(shard, 1, 2)
    ahead, behind = jnp.where(one == two, up2, dn2), jnp.where(one == two, dn2, up2)
    up3, dn3 = swap(behind, 0, 1), swap(ahead, 1, 1)
    return shard, up1, dn1, up2, dn2, dn3, up3, swap(dn2, 0, 2)


def scatter_y(own, up1, dn1, up2, dn2, dn3, up3, far):
    one, two = sides()
    far = swap(far, 0, 2)
    behind, ahead = swap(up3, 0, 1), swap(dn3, 1, 1)
    up2 = add(up2, jnp.where(one == two, ahead, behind))
    dn2 = add(dn2, jnp.where(one == two, behind, ahead), far)
    parts = swap(up1, 0, 1), swap(dn1, 1, 1), swap(up2, 0, 2), swap(dn2, 1, 2)
    (out,) = call(last_kernel, (own, *parts), [((LANES, WIDTH), BF16)])
    return out


def y_sums(part):
    return lax.all_to_all(part, "y", 0, 0)


def group_sums(part, dtype):
    part = (part + shift(part, "core", CORES, 1)).astype(dtype)
    part = jnp.broadcast_to(part[None], (GROUP,) + part.shape)
    return lax.all_to_all(part, ("z", "x"), 0, 0)


def on_device(embeddings, prototypes):
    mine = embeddings.transpose(1, 0, 2)
    as_given = Layout(major_to_minor=(0, 1, 2))
    theirs = shift(with_layout_constraint(embeddings, as_given), "core", CORES, 1)
    theirs = with_layout_constraint(theirs, as_given).transpose(1, 0, 2)
    pieces = gather_y(prototypes)
    rows, flat = call(
        rows_kernel,
        (mine, theirs),
        [((VIEWS, ROWS, WIDTH), BF16), ((WIDTH, VIEWS * ROWS), BF16)],
    )
    cols, rows8, rows16 = ((16, LANES), F32), ((8, LANES), F32), ((16, LANES), F32)
    col_out = ((YS, 16, LANES), BF16)
    row_out = ((8, LANES), F32)
    both_out = ((16, LANES), F32)
    work = 4 * ROWS * WIDTH
    early, col_part, soft, near_centers = call(
        early_kernel, (rows, *pieces[:EARLY]),
        [((VIEWS, ROWS, SPLIT), F32), cols, rows8, ((SPLIT, WIDTH), BF16)], (), work * SPLIT,
    )
    late, col_part, soft, far_centers = call(
        late_kernel, (rows, *pieces[EARLY:], col_part, soft),
        [((VIEWS, ROWS, COLS - SPLIT), F32), col_out, rows8, ((COLS - SPLIT, WIDTH), BF16)],
        [cols, rows8], work * (COLS - SPLIT),
    )
    col_part = y_sums(col_part)
    (row_part,) = call(
        functools.partial(row_kernel, True), (early, late, col_part, soft), [both_out],
        [cols, rows8],
    )
    row_part = group_sums(row_part, BF16)
    col_part, soft = call(
        functools.partial(col_kernel, True), (early, late, row_part), [col_out, rows8],
        [rows16, cols],
    )
    col_part = y_sums(col_part)
    (row_part,) = call(
        functools.partial(row_kernel, False), (early, late, col_part), [row_out], [cols, rows8]
    )
    row_part = group_sums(row_part, BF16)
    (col_part,) = call(
        functools.partial(col_kernel, False), (early, late, row_part), [col_out], [rows8, cols]
    )
    col_part = y_sums(col_part)
    (row_part,) = call(
        functools.partial(row_kernel, False), (early, late, col_part), [row_out], [cols, rows8]
    )
    row_part = group_sums(row_part, BF16)

    ge_out = ((XS * ZS, 16, WIDTH), BF16)
    mine, other, grads = call(
        grad_kernel,
        (early, late, row_part, col_part, soft, near_centers, far_centers),
        [ge_out, ge_out, ((VIEWS * ROWS, COLS), BF16)], [cols, rows8], work * COLS,
    )
    sums = call(
        proto_kernel, (flat, grads), [((WIDTH, LANES), BF16)] * SLOTS, (), work * COLS
    )
    theirs = shift(other, "core", CORES, 1)
    mine, sums = lax.optimization_barrier((mine, sums))
    part = add(mine, theirs)
    part = lax.all_to_all(part, ("z", "x"), 0, 0)
    part = jnp.sum(part.astype(F32), axis=0).astype(BF16)
    grad_embed = part.reshape(2, 8, WIDTH).transpose(1, 0, 2)
    own, grad_embed = lax.optimization_barrier((sums[0], grad_embed))
    return grad_embed, scatter_y(own, *sums[1:])


def solution(mesh):
    split = Mesh(mesh.devices.reshape(YS, CORES, XS, ZS), ("y", "core", "x", "z"))
    batch, every = ("y", "core"), ("y", "core", "x", "z")
    return jax.shard_map(
        on_device,
        mesh=split,
        in_specs=(P(batch, None, None), P(every, None)),
        out_specs=(P(every, None, None), P(every, None)),
        check_vma=False,
    )
```
